512 devices in a mesh: ctx: 64 (over x, y_hi, z), tp: 8 (over y_lo, core).
Axes of the slice: x: 4, y: 8 (y_hi: 2, y_lo: 4; y = y_hi * 4 + y_lo), z: 8, core: 2. Of those that a mesh axis runs over, the one named last changes fastest.
Arguments:
- inputs: float32 [64, 2, 64, 2048], P('ctx', None, None, 'tp'), may hold values from -0.3 to 0.3
- b_matrix: float32 [64, 2, 64, 1024], P('ctx', None, None, 'tp'), may hold values from -1.2 to 1.2
- c_matrix: float32 [64, 2, 64, 1024], P('ctx', None, None, 'tp'), may hold values from -1.2 to 1.2
- step_sizes: float32 [64, 2, 64, 64], P('ctx', None, 'tp'), may hold values from 0.3 to 8192, as said below
- decay_rate: float32 [64], P('tp'), as said below
- cotangent: float32 [64, 2, 64, 2048], P('ctx', None, None, 'tp'), may hold values from -7.5 to 7.5
Outputs:
- grad_inputs: float32 [64, 2, 64, 2048], P('ctx', None, None, 'tp')
- grad_b: float32 [64, 2, 64, 1024], P('ctx', None, None, 'tp')
- grad_c: float32 [64, 2, 64, 1024], P('ctx', None, None, 'tp')
- grad_steps: float32 [64, 2, 64, 64], P('ctx', None, 'tp')
The draws below stay inside these ranges and needn't reach their ends.
Inputs may be any that keep to these rules, and one draw needn't show every extreme that they name: `decay_rate`: each head's rate is positive. `step_sizes`: steps are positive.
All inputs are finite; a program needn't handle non-finite values.
Results may differ from the reference program's by a relative error of at most 0.0003.
Values sent between devices are 32-bit elements; how exact they have to be, the bound alone decides.
A program may use at most 128 MiB of HBM per device.

```python
import math
import jax
import jax.numpy as jnp
from jax import lax

HEADS = 64
HEAD_DIM = 32
STATE = 128
GROUPS = 8
HALF = 64
SPLITS = 64
SEQUENCE_LENGTH = 8192


def draw_decay_rate(key, part):
    key = jax.random.fold_in(key, 11)
    key_order, key_offset, key_slow = jax.random.split(key, 3)
    fast_count = max(HEADS // 2, 1)
    ranking = jax.random.permutation(key_order, HEADS)
    offset = jax.random.uniform(key_offset, (HEADS,), jnp.float32, 0.0, 1.0)
    position = (ranking.astype(jnp.float32) + offset) / fast_count
    fast_rate = jnp.exp(math.log(0.0012) + position * math.log(0.04 / 0.0012))
    slow_rate = jnp.exp(jax.random.uniform(key_slow, (HEADS,), jnp.float32, math.log(1.2), math.log(2.4))) / SEQUENCE_LENGTH
    return jnp.where(ranking < fast_count, fast_rate, slow_rate).astype(jnp.float32)


def draw_step_sizes(key, part):
    key = jax.random.fold_in(key, 23)
    key_base, key_factor, key_spots, random_key_values = jax.random.split(key, 4)
    shape = (SPLITS, 2, HEADS, HALF)
    base = jnp.exp(jax.random.uniform(key_base, shape, jnp.float32, math.log(0.5), math.log(2.0)))
    factor = jnp.exp(jax.random.uniform(key_factor, (SPLITS, 2, HEADS, 1), jnp.float32, math.log(0.6), math.log(1.6)))
    location_sequence = jax.random.randint(key_spots, (2,), 0, SPLITS * 2 * HALF)
    spike_values = jax.random.uniform(random_key_values, (2,), jnp.float32, 0.5, 0.8) * SEQUENCE_LENGTH
    pair_ids = jax.lax.broadcasted_iota(jnp.int32, (SPLITS, 2, 1, HALF), 0)
    slot_ids = jax.lax.broadcasted_iota(jnp.int32, (SPLITS, 2, 1, HALF), 1)
    place_ids = jax.lax.broadcasted_iota(jnp.int32, (SPLITS, 2, 1, HALF), 3)
    flat_offset = (pair_ids * 2 + slot_ids) * HALF + place_ids
    uniform_steps = base * factor
    merged_result = jnp.where(flat_offset == location_sequence[0], spike_values[0], jnp.where(flat_offset == location_sequence[1], spike_values[1], uniform_steps))
    return merged_result.astype(jnp.float32)


def block_scale(rng, extent, cuts, smallest, high):
    gain = 1.0
    for axis_at, blocks in cuts:
        steps = jax.random.uniform(jax.random.fold_in(jax.random.fold_in(rng, 6), axis_at), (blocks,), jnp.float32, smallest / len(cuts), high / len(cuts))
        gain = gain * jnp.repeat(jnp.exp(steps), extent[axis_at] // blocks).reshape((-1,) + (1,) * (len(extent) - 1 - axis_at))
    return gain


def centred(rng, extent, scale, bound, cuts=(), dtype=jnp.bfloat16):
    values = scale * jax.random.normal(rng, extent, jnp.float32)
    if cuts:
        values = values * block_scale(rng, extent, cuts, -0.22, 0.18)
    return jnp.clip(values, -bound, bound).astype(dtype)


def setup_inputs(seed: int = 0) -> dict:
    key_of = jax.random.split(jax.random.key(seed), 7)
    return {
        "inputs": centred(key_of[0], (SPLITS, 2, HALF, HEADS * HEAD_DIM), 0.05, 0.3, ((0, 64), (3, 8)), jnp.float32),
        "b_matrix": centred(key_of[1], (SPLITS, 2, HALF, GROUPS * STATE), 0.2, 1.2, ((0, 64), (3, 8)), jnp.float32),
        "c_matrix": centred(key_of[2], (SPLITS, 2, HALF, GROUPS * STATE), 0.2, 1.2, ((0, 64), (3, 8)), jnp.float32),
        "step_sizes": draw_step_sizes(jax.random.fold_in(key_of[6], 71), 0),
        "decay_rate": draw_decay_rate(jax.random.fold_in(key_of[6], 71), 0),
        "cotangent": centred(key_of[5], (SPLITS, 2, HALF, HEADS * HEAD_DIM), 1.25, 7.5, ((0, 64), (3, 8)), jnp.float32),
    }


HIGHEST = lax.Precision.HIGHEST

def half_pass(inputs_h, b_block, c_block, step_block, decay_rate, state_in):
    head_count = step_block.shape[0]
    length = step_block.shape[1]
    head_width = state_in.shape[1]
    state_width = state_in.shape[2]
    group_count = b_block.shape[1] // state_width
    per_group = head_count // group_count
    log_decay = -decay_rate[:, None] * step_block
    cumulative = jnp.cumsum(log_decay, axis=1)
    row_ids = lax.broadcasted_iota(jnp.int32, (length, length), 0)
    col_ids = lax.broadcasted_iota(jnp.int32, (length, length), 1)
    causal = row_ids >= col_ids
    b_three = b_block.reshape(length, group_count, state_width)
    c_three = c_block.reshape(length, group_count, state_width)
    scores = jnp.einsum('tgn,sgn->gts', c_three, b_three, precision=HIGHEST)
    decays = jnp.exp(jnp.where(causal[None], cumulative[:, :, None] - cumulative[:, None, :], -jnp.inf))
    weights = scores[:, None] * decays.reshape(group_count, per_group, length, length)
    per_head = inputs_h.reshape(length, group_count, per_group, head_width)
    inner_portion = jnp.einsum('gkts,sgkp->tgkp', weights, per_head, precision=HIGHEST)
    state_four = state_in.reshape(group_count, per_group, head_width, state_width)
    growth = jnp.exp(cumulative).T.reshape(length, group_count, per_group, 1)
    carried = jnp.einsum('tgn,gkpn->tgkp', c_three, state_four, precision=HIGHEST) * growth
    to_end = jnp.exp(cumulative[:, -1:] - cumulative).T.reshape(length, group_count, per_group, 1)
    weighted = per_head * to_end
    fresh = jnp.einsum('sgkp,sgn->gkpn', weighted, b_three, precision=HIGHEST).reshape(head_count, head_width, state_width)
    state_out = jnp.exp(cumulative[:, -1])[:, None, None] * state_in + fresh
    return ((inner_portion + carried).reshape(length, head_count * head_width), state_out)

def to_sequence(array):
    return jnp.concatenate([array[:, 0], array[::-1, 1]], axis=0)

def reference(inputs, b_matrix, c_matrix, step_sizes, decay_rate, cotangent):

    def objective(x_array, b_array, readout_tensor, s_array):
        pieces_all = (to_sequence(x_array), to_sequence(b_array), to_sequence(readout_tensor), to_sequence(s_array), to_sequence(cotangent))

        def advance(hidden_state, pieces):
            x_block, b_block, c_block, step_block, cotan_block = pieces
            output, new_state = half_pass(x_block, b_block, c_block, step_block, decay_rate, hidden_state)
            return (new_state, jnp.sum(output * cotan_block))
        initial = jnp.zeros((HEADS, HEAD_DIM, STATE), jnp.float32)
        _, partial_sums = lax.scan(jax.checkpoint(advance), initial, pieces_all)
        return jnp.sum(partial_sums)
    grad_inputs, grad_b, grad_c, grad_steps = jax.grad(objective, argnums=(0, 1, 2, 3))(inputs, b_matrix, c_matrix, step_sizes)
    return (grad_inputs, grad_b, grad_c, grad_steps)
```

```python
import functools

import jax
import jax.numpy as jnp
from jax import lax
from jax.experimental import pallas as pl
from jax.experimental.pallas import tpu as pltpu
from jax.sharding import PartitionSpec as P

F32 = jnp.float32
BF16 = jnp.bfloat16
HIGHEST = lax.Precision.HIGHEST
MESH = pl.DeviceIdType.MESH

N = 64
T = 64
H = 8
PW = 32
W = H * PW
S = 128

NN = (((1,), (0,)), ((), ()))
NT = (((1,), (1,)), ((), ()))
TN = (((0,), (0,)), ((), ()))


def split(a):
    high = a.astype(BF16)
    low = (a - high.astype(F32)).astype(BF16)
    return high, low


def dot(a, b, dims=NN):
    return lax.dot_general(a, b, dims, preferred_element_type=F32)


def mm(a, b, dims=NN):
    return dot(a[0], b[0], dims) + (dot(a[0], b[1], dims) + dot(a[1], b[0], dims))


def exact(a, b, dims=NN):
    return lax.dot_general(a, b, dims, precision=HIGHEST, preferred_element_type=F32)


def iota(shape, dim):
    return lax.broadcasted_iota(jnp.int32, shape, dim)


def kernel(
    x_ref, b_ref, c_ref, st_ref, rate_ref, g_ref,
    gx_ref, gb_ref, gc_ref, gs_ref,
    dec, decs, tiles, send_s, send_a, recv_s, recv_a, out_s, out_a, in_s, in_a,
    sems, rems,
):
    me = lax.axis_index("ctx")
    px, py, pz = me // 16, (me // 8) % 2, me % 8

    def peer(o):
        dx, dy, dz = o % 4, (o // 4) % 2, o // 8
        return ((px + dx) % 4) * 16 + ((py + dy) % 2) * 8 + (pz + dz) % 8

    barrier = pltpu.get_barrier_semaphore()

    def greet(i, carry):
        pl.semaphore_signal(
            barrier, inc=1, device_id={"ctx": peer(N - 1 - i)}, device_id_type=MESH
        )
        return carry

    lax.fori_loop(0, N - 1, greet, 0, unroll=7)

    def send_all(source, target, which, at):
        def one(i, carry):
            to = peer(N - 1 - i)
            pltpu.make_async_remote_copy(
                src_ref=source.at[at(to)],
                dst_ref=target.at[me],
                send_sem=sems.at[which],
                recv_sem=rems.at[which],
                device_id={"ctx": to},
                device_id_type=MESH,
            ).start()
            return carry

        lax.fori_loop(0, N - 1, one, 0, unroll=7)

    def wait_all(sem, which, like):
        some = like.at[pl.ds(0, N - 1)]
        pltpu.make_async_copy(some, some, sem.at[which]).wait()

    head = iota((H, T), 0)
    rate = jnp.zeros((H, T), F32)
    for h in range(H):
        rate = jnp.where(head == h, rate_ref[h], rate)
    row_t, col_t = iota((T, T), 0), iota((T, T), 1)
    tri = (col_t <= row_t).astype(F32)
    sel32 = (iota((H, W), 1) // PW == iota((H, W), 0)).astype(F32)
    cum, spread, from_start, to_end = [], [], [], []
    for i in range(2):
        logd = -rate * st_ref[0, i]
        total = jnp.exp(jnp.sum(logd, axis=1, keepdims=True))
        for h in range(H):
            dec[h, pl.ds(i, 1), :] = jnp.broadcast_to(total[h : h + 1], (1, S))
        cum_i = exact(tri, logd, NT)
        wide = exact(cum_i, sel32)
        cum.append(cum_i)
        spread.append(wide)
        from_start.append(jnp.exp(wide))
        to_end.append(jnp.exp(wide[T - 1 : T] - wide))
    decs[me] = dec[me // 8]

    low_half = iota((8, S), 0) < 4
    xw, gw, bs, cs, xs, gs = [], [], [], [], [], []

    def pack(first, second, buffer):
        for k in range(N // 2):
            one, two = first[8 * k : 8 * k + 8], second[8 * k : 8 * k + 8]
            buffer[2 * k] = jnp.where(low_half, one, pltpu.roll(two, 4, 0))
            buffer[2 * k + 1] = jnp.where(low_half, pltpu.roll(one, 4, 0), two)

    for i in range(2):
        x, b = x_ref[0, i], b_ref[0, i]
        xs.append(split(x))
        bs.append(split(b))
        xw.append(split(x * to_end[i]))
    state = [mm(xw[i], bs[i], TN) for i in range(2)]
    pack(state[0], state[1], send_s)
    recv_s[me] = send_s[me]

    pl.semaphore_wait(barrier, N - 1)
    send_all(dec, decs, 0, lambda to: to // 8)
    send_all(send_s, recv_s, 1, lambda to: to)

    for i in range(2):
        g, c = g_ref[0, i], c_ref[0, i]
        gs.append(split(g))
        cs.append(split(c))
        gw.append(split(g * from_start[i]))
    adjoint = [mm(gw[i], cs[i], TN) for i in range(2)]
    pack(adjoint[0], adjoint[1], send_a)
    recv_a[me] = send_a[me]
    send_all(send_a, recv_a, 2, lambda to: to)

    lane_head = iota((T, W), 1) // PW
    t_wide, s_wide = iota((T, H * T), 0), iota((T, H * T), 1) % T
    sel64 = (iota((H, H * T), 1) // T == iota((H, H * T), 0)).astype(F32)
    pick = (iota((H * T, H), 0) // T == iota((H * T, H), 1)).astype(BF16)
    pick32 = (iota((W, H), 0) // PW == iota((W, H), 1)).astype(BF16)
    zero = jnp.zeros((), BF16)

    def stacked(parts):
        return [
            jnp.concatenate([jnp.where(lane_head == h, part, zero) for h in range(H)], axis=0)
            for part in parts
        ]

    def twice(parts):
        return [jnp.concatenate([part, part], axis=0) for part in parts]

    def folded(a):
        return a[:, :128] + a[:, 128:256] + (a[:, 256:384] + a[:, 384:])

    def by_head(a, selection):
        high, low = split(a)
        return dot(high, selection) + dot(low, selection)

    def within(i):
        columns = exact(cum[i], sel64)
        row = jnp.sum(jnp.where(t_wide == s_wide, columns, 0.0), axis=0, keepdims=True)
        gap = columns - row
        forward = jnp.exp(jnp.where(s_wide <= t_wide, gap, -1e30))
        backward = jnp.exp(jnp.where(s_wide >= t_wide, -gap, -1e30))
        b_twice, c_twice = twice(bs[i]), twice(cs[i])
        x_stack, g_stack = stacked(xs[i]), stacked(gs[i])
        scores = jnp.concatenate([mm(cs[i], b_twice, NT)] * 4, axis=1)
        scores_back = jnp.concatenate([mm(bs[i], c_twice, NT)] * 4, axis=1)
        inner = forward * mm(gs[i], x_stack, NT)
        inner_back = backward * mm(xs[i], g_stack, NT)
        gc_ref[0, i] = mm(split(folded(inner)), b_twice)
        gb_ref[0, i] = mm(split(folded(inner_back)), c_twice)
        gx_ref[0, i] = mm(split(scores_back * backward), g_stack)
        off = s_wide != t_wide
        return by_head(jnp.where(off, scores * inner, 0.0), pick) - by_head(
            jnp.where(off, scores_back * inner_back, 0.0), pick
        )

    d_cum = [within(0), None]

    def scan(received, result, low_first):
        keep = low_half if low_first else jnp.logical_not(low_half)

        def up(j, carry):
            result[j] = carry
            return tiles[j] * carry + received[j]

        top = lax.fori_loop(0, N, up, jnp.zeros((8, S), F32), unroll=8)

        def down(i, carry):
            j = N - 1 - i
            result[j] = jnp.where(keep, result[j], carry)
            return tiles[j] * carry + received[j]

        lax.fori_loop(0, N, down, pltpu.roll(top, 4, 0), unroll=8)

    wait_all(rems, 0, decs)

    def spread_decay(j, carry):
        tiles[j] = jnp.where(low_half, decs[j, 0:1, :], decs[j, 1:2, :])
        return carry

    lax.fori_loop(0, N, spread_decay, 0, unroll=8)
    wait_all(rems, 1, recv_s)
    scan(recv_s, out_s, True)
    in_s[me] = out_s[me]
    send_all(out_s, in_s, 3, lambda to: to)
    wait_all(rems, 2, recv_a)
    scan(recv_a, out_a, False)
    in_a[me] = out_a[me]
    send_all(out_a, in_a, 4, lambda to: to)

    d_cum[1] = within(1)

    def unpack(buffer):
        first, second = [], []
        for k in range(N // 2):
            one, two = buffer[2 * k], buffer[2 * k + 1]
            first.append(jnp.where(low_half, one, pltpu.roll(two, 4, 0)))
            second.append(jnp.where(low_half, pltpu.roll(one, 4, 0), two))
        return jnp.concatenate(first, axis=0), jnp.concatenate(second, axis=0)

    wait_all(rems, 3, in_s)
    entering = unpack(in_s)
    for i in range(2):
        parts = split(entering[i])
        carried = mm(cs[i], parts, NT)
        gc_ref[0, i] += mm(gw[i], parts)
        d_cum[i] += by_head(g_ref[0, i] * from_start[i] * carried, pick32)
    wait_all(rems, 4, in_a)
    leaving = unpack(in_a)
    after = (row_t >= col_t).astype(F32)
    before = (row_t < col_t).astype(F32)
    for i in range(2):
        parts = split(leaving[i])
        weighted = to_end[i] * mm(bs[i], parts, NT)
        gx_ref[0, i] += weighted
        gb_ref[0, i] += mm(xw[i], parts)
        fresh = by_head(x_ref[0, i] * weighted, pick32)
        ends = exact(sel32, leaving[i] * entering[i])
        through = jnp.sum(ends, axis=1, keepdims=True) * jnp.concatenate(
            [dec[h, pl.ds(i, 1), 0:1] for h in range(H)], axis=0
        )
        d_log = exact(d_cum[i], after, TN) + exact(fresh, before, TN) + through
        gs_ref[0, i] = -rate * d_log

    wait_all(sems, 0, decs)
    wait_all(sems, 1, send_s)
    wait_all(sems, 2, send_a)
    wait_all(sems, 3, out_s)
    wait_all(sems, 4, out_a)


def per_device(inputs, b_matrix, c_matrix, step_sizes, decay_rate, cotangent):
    vmem = pl.BlockSpec(memory_space=pltpu.VMEM)
    smem = pl.BlockSpec(memory_space=pltpu.SMEM)
    chunks = pltpu.VMEM((N, 8, S), F32)
    return pl.pallas_call(
        kernel,
        name="mirrored_scan",
        out_shape=[
            jax.ShapeDtypeStruct(a.shape, F32) for a in (inputs, b_matrix, c_matrix, step_sizes)
        ],
        in_specs=[vmem, vmem, vmem, vmem, smem, vmem],
        out_specs=[vmem] * 4,
        scratch_shapes=[
            pltpu.VMEM((H, 2, S), F32),
            pltpu.VMEM((N, 2, S), F32),
            *[chunks] * 9,
            pltpu.SemaphoreType.DMA((5,)),
            pltpu.SemaphoreType.DMA((5,)),
        ],
        compiler_params=pltpu.CompilerParams(
            collective_id=0, has_side_effects=True, vmem_limit_bytes=40 << 20
        ),
    )(inputs, b_matrix, c_matrix, step_sizes, decay_rate, cotangent)


def solution(mesh):
    blocks = P("ctx", None, None, "tp")
    steps = P("ctx", None, "tp", None)
    return jax.shard_map(
        per_device,
        mesh=mesh,
        in_specs=(blocks, blocks, blocks, steps, P("tp"), blocks),
        out_specs=(blocks, blocks, blocks, steps),
        check_vma=False,
    )
```

```python
import functools

import jax
import jax.numpy as jnp
from jax import lax
from jax.experimental import pallas as pl
from jax.experimental.pallas import tpu as pltpu
from jax.sharding import PartitionSpec as P

F32 = jnp.float32
BF16 = jnp.bfloat16
HIGHEST = lax.Precision.HIGHEST
MESH = pl.DeviceIdType.MESH

N = 64
T = 64
H = 8
PW = 32
W = H * PW
S = 128

NN = (((1,), (0,)), ((), ()))
NT = (((1,), (1,)), ((), ()))
TN = (((0,), (0,)), ((), ()))


def split(a):
    high = a.astype(BF16)
    low = (a - high.astype(F32)).astype(BF16)
    return high, low


def dot(a, b, dims=NN):
    return lax.dot_general(a, b, dims, preferred_element_type=F32)


def mm(a, b, dims=NN):
    return dot(a[0], b[0], dims) + (dot(a[0], b[1], dims) + dot(a[1], b[0], dims))


def exact(a, b, dims=NN):
    return lax.dot_general(a, b, dims, precision=HIGHEST, preferred_element_type=F32)


def iota(shape, dim):
    return lax.broadcasted_iota(jnp.int32, shape, dim)


def kernel(
    x_any, b_any, c_any, st_any, rate_any, g_any,
    gx_ref, gb_ref, gc_ref, gs_ref,
    x_ref, b_ref, c_ref, st_ref, rate_ref, g_ref,
    dec, decs, tiles, send_s, send_a, recv_s, recv_a, out_s, out_a, in_s, in_a,
    sems, rems, loads,
):
    me = lax.axis_index("ctx")
    px, py, pz = me // 16, (me // 8) % 2, me % 8
    x_part = [lax.rem(px + k, 4) * 16 for k in range(4)]
    y_part = [lax.rem(py + k, 2) * 8 for k in range(2)]
    z_part = [lax.rem(pz + k, 8) for k in range(8)]
    peers = [
        x_part[x] + y_part[y] + z_part[z]
        for z in (4, 3, 5, 2, 6, 1, 7, 0)
        for y in (1, 0)
        for x in (2, 1, 3, 0)
    ][:-1]

    barrier = pltpu.get_barrier_semaphore()

    for to in peers:
        pl.semaphore_signal(barrier, inc=1, device_id={"ctx": to}, device_id_type=MESH)

    operands = (
        (st_any, st_ref), (rate_any, rate_ref), (x_any, x_ref), (b_any, b_ref),
        (g_any, g_ref), (c_any, c_ref),
    )
    copies = [
        pltpu.make_async_copy(there, here, loads.at[k]) for k, (there, here) in enumerate(operands)
    ]
    for copy in copies:
        copy.start()

    def send(source, target, which, to):
        pltpu.make_async_remote_copy(
            src_ref=source,
            dst_ref=target,
            send_sem=sems.at[which],
            recv_sem=rems.at[which],
            device_id={"ctx": to},
            device_id_type=MESH,
        ).start()

    def send_all(source, target, which):
        for to in peers:
            send(source.at[to], target.at[me], which, to)

    def wait_all(sem, which, like):
        some = like.at[pl.ds(0, like.shape[0] - 1)]
        pltpu.make_async_copy(some, some, sem.at[which]).wait()

    copies[0].wait()
    copies[1].wait()
    head = iota((H, T), 0)
    rate = jnp.zeros((H, T), F32)
    for h in range(H):
        rate = jnp.where(head == h, rate_ref[h], rate)
    row_t, col_t = iota((T, T), 0), iota((T, T), 1)
    tri = (col_t <= row_t).astype(F32)
    sel32 = (iota((H, W), 1) // PW == iota((H, W), 0)).astype(F32)
    cum, spread, from_start, to_end = [], [], [], []
    for i in range(2):
        logd = -rate * st_ref[0, i]
        total = jnp.exp(jnp.sum(logd, axis=1, keepdims=True))
        for h in range(H):
            dec[h, pl.ds(i, 1), :] = jnp.broadcast_to(total[h : h + 1], (1, S))
        cum_i = exact(tri, logd, NT)
        wide = exact(cum_i, sel32)
        cum.append(cum_i)
        spread.append(wide)
        from_start.append(jnp.exp(wide))
        to_end.append(jnp.exp(wide[T - 1 : T] - wide))
    decs[me] = dec[me // 8]

    low_half = iota((8, S), 0) < 4
    xw, gw, bs, cs, xs, gs = [], [], [], [], [], []

    def pack(first, second, buffer):
        for k in range(N // 2):
            one, two = first[8 * k : 8 * k + 8], second[8 * k : 8 * k + 8]
            buffer[2 * k] = jnp.where(low_half, one, pltpu.roll(two, 4, 0))
            buffer[2 * k + 1] = jnp.where(low_half, pltpu.roll(one, 4, 0), two)

    copies[2].wait()
    copies[3].wait()
    for i in range(2):
        x, b = x_ref[0, i], b_ref[0, i]
        xs.append(split(x))
        bs.append(split(b))
        xw.append(split(x * to_end[i]))
    state = [mm(xw[i], bs[i], TN) for i in range(2)]
    pack(state[0], state[1], send_s)
    recv_s[me] = send_s[me]

    pl.semaphore_wait(barrier, N - 1)
    for to in peers:
        send(dec.at[to // 8], decs.at[me], 0, to)
    send_all(send_s, recv_s, 1)

    copies[4].wait()
    copies[5].wait()
    for i in range(2):
        g, c = g_ref[0, i], c_ref[0, i]
        gs.append(split(g))
        cs.append(split(c))
        gw.append(split(g * from_start[i]))
    adjoint = [mm(gw[i], cs[i], TN) for i in range(2)]
    pack(adjoint[0], adjoint[1], send_a)
    recv_a[me] = send_a[me]
    send_all(send_a, recv_a, 2)

    lane_head = iota((T, W), 1) // PW
    t_wide, s_wide = iota((T, H * T), 0), iota((T, H * T), 1) % T
    sel64 = (iota((H, H * T), 1) // T == iota((H, H * T), 0)).astype(F32)
    pick = (iota((H * T, H), 0) // T == iota((H * T, H), 1)).astype(BF16)
    pick32 = (iota((W, H), 0) // PW == iota((W, H), 1)).astype(BF16)
    zero = jnp.zeros((), BF16)

    def stacked(parts):
        return [
            jnp.concatenate([jnp.where(lane_head == h, part, zero) for h in range(H)], axis=0)
            for part in parts
        ]

    def twice(parts):
        return [jnp.concatenate([part, part], axis=0) for part in parts]

    def folded(a):
        return a[:, :128] + a[:, 128:256] + (a[:, 256:384] + a[:, 384:])

    def by_head(a, selection):
        high, low = split(a)
        return dot(high, selection) + dot(low, selection)

    def within(i):
        columns = exact(cum[i], sel64)
        row = jnp.sum(jnp.where(t_wide == s_wide, columns, 0.0), axis=0, keepdims=True)
        gap = columns - row
        forward = jnp.exp(jnp.where(s_wide <= t_wide, gap, -1e30))
        backward = jnp.exp(jnp.where(s_wide >= t_wide, -gap, -1e30))
        b_twice, c_twice = twice(bs[i]), twice(cs[i])
        x_stack, g_stack = stacked(xs[i]), stacked(gs[i])
        scores = jnp.concatenate([mm(cs[i], b_twice, NT)] * 4, axis=1)
        scores_back = jnp.concatenate([mm(bs[i], c_twice, NT)] * 4, axis=1)
        inner = forward * mm(gs[i], x_stack, NT)
        inner_back = backward * mm(xs[i], g_stack, NT)
        gc_ref[0, i] = mm(split(folded(inner)), b_twice)
        gb_ref[0, i] = mm(split(folded(inner_back)), c_twice)
        gx_ref[0, i] = mm(split(scores_back * backward), g_stack)
        off = s_wide != t_wide
        return by_head(jnp.where(off, scores * inner, 0.0), pick) - by_head(
            jnp.where(off, scores_back * inner_back, 0.0), pick
        )

    d_cum = [within(0), None]

    def scan(received, result, low_first):
        keep = low_half if low_first else jnp.logical_not(low_half)

        def up(j, carry):
            result[j] = carry
            return tiles[j] * carry + received[j]

        top = lax.fori_loop(0, N, up, jnp.zeros((8, S), F32), unroll=8)

        def down(i, carry):
            j = N - 1 - i
            result[j] = jnp.where(keep, result[j], carry)
            return tiles[j] * carry + received[j]

        lax.fori_loop(0, N, down, pltpu.roll(top, 4, 0), unroll=8)

    wait_all(rems, 0, decs)

    def spread_decay(j, carry):
        tiles[j] = jnp.where(low_half, decs[j, 0:1, :], decs[j, 1:2, :])
        return carry

    lax.fori_loop(0, N, spread_decay, 0, unroll=8)
    wait_all(rems, 1, recv_s)
    scan(recv_s, out_s, True)
    in_s[me] = out_s[me]
    send_all(out_s, in_s, 3)
    wait_all(rems, 2, recv_a)
    scan(recv_a, out_a, False)
    in_a[me] = out_a[me]
    send_all(out_a, in_a, 4)

    d_cum[1] = within(1)

    def unpack(buffer):
        first, second = [], []
        for k in range(N // 2):
            one, two = buffer[2 * k], buffer[2 * k + 1]
            first.append(jnp.where(low_half, one, pltpu.roll(two, 4, 0)))
            second.append(jnp.where(low_half, pltpu.roll(one, 4, 0), two))
        return jnp.concatenate(first, axis=0), jnp.concatenate(second, axis=0)

    wait_all(rems, 3, in_s)
    entering = unpack(in_s)
    for i in range(2):
        parts = split(entering[i])
        carried = mm(cs[i], parts, NT)
        gc_ref[0, i] += mm(gw[i], parts)
        d_cum[i] += by_head(g_ref[0, i] * from_start[i] * carried, pick32)
    wait_all(rems, 4, in_a)
    leaving = unpack(in_a)
    after = (row_t >= col_t).astype(F32)
    before = (row_t < col_t).astype(F32)
    for i in range(2):
        parts = split(leaving[i])
        weighted = to_end[i] * mm(bs[i], parts, NT)
        gx_ref[0, i] += weighted
        gb_ref[0, i] += mm(xw[i], parts)
        fresh = by_head(x_ref[0, i] * weighted, pick32)
        ends = exact(sel32, leaving[i] * entering[i])
        through = jnp.sum(ends, axis=1, keepdims=True) * jnp.concatenate(
            [dec[h, pl.ds(i, 1), 0:1] for h in range(H)], axis=0
        )
        d_log = exact(d_cum[i], after, TN) + exact(fresh, before, TN) + through
        gs_ref[0, i] = -rate * d_log

    wait_all(sems, 0, decs)
    wait_all(sems, 1, send_s)
    wait_all(sems, 2, send_a)
    wait_all(sems, 3, out_s)
    wait_all(sems, 4, out_a)


def leave(*refs):
    n = len(refs) // 2
    copies = [
        pltpu.make_async_copy(here, there, refs[-1].at[k])
        for k, (here, there) in enumerate(zip(refs[:n], refs[n : 2 * n]))
    ]
    for copy in copies:
        copy.start()
    for copy in copies:
        copy.wait()


def per_device(inputs, b_matrix, c_matrix, step_sizes, decay_rate, cotangent):
    vmem = pl.BlockSpec(memory_space=pltpu.VMEM)
    hbm = pl.BlockSpec(memory_space=pltpu.HBM)
    chunks = pltpu.VMEM((N, 8, S), F32)
    outs = [jax.ShapeDtypeStruct(a.shape, F32) for a in (inputs, b_matrix, c_matrix, step_sizes)]
    results = pl.pallas_call(
        kernel,
        name="mirrored_scan",
        out_shape=outs,
        in_specs=[hbm] * 6,
        out_specs=[vmem] * 4,
        scratch_shapes=[
            *[pltpu.VMEM(a.shape, F32) for a in (inputs, b_matrix, c_matrix, step_sizes)],
            pltpu.SMEM(decay_rate.shape, F32),
            pltpu.VMEM(cotangent.shape, F32),
            pltpu.VMEM((H, 2, S), F32),
            pltpu.VMEM((N, 2, S), F32),
            *[chunks] * 9,
            pltpu.SemaphoreType.DMA((5,)),
            pltpu.SemaphoreType.DMA((5,)),
            pltpu.SemaphoreType.DMA((6,)),
        ],
        compiler_params=pltpu.CompilerParams(
            collective_id=0, has_side_effects=True, vmem_limit_bytes=60 << 20
        ),
    )(inputs, b_matrix, c_matrix, step_sizes, decay_rate, cotangent)
    return pl.pallas_call(
        leave,
        name="leave",
        out_shape=results,
        in_specs=[vmem] * 4,
        out_specs=[hbm] * 4,
        scratch_shapes=[pltpu.SemaphoreType.DMA((4,))],
    )(*results)


def solution(mesh):
    blocks = P("ctx", None, None, "tp")
    steps = P("ctx", None, "tp", None)
    return jax.shard_map(
        per_device,
        mesh=mesh,
        in_specs=(blocks, blocks, blocks, steps, P("tp"), blocks),
        out_specs=(blocks, blocks, blocks, steps),
        check_vma=False,
    )
```

```python
import functools

import jax
import jax.numpy as jnp
from jax import lax
from jax.experimental import pallas as pl
from jax.experimental.pallas import tpu as pltpu
from jax.sharding import PartitionSpec as P

F32 = jnp.float32
BF16 = jnp.bfloat16
HIGHEST = lax.Precision.HIGHEST
MESH = pl.DeviceIdType.MESH

N = 32
X, Z = 4, 8
T = 64
H = 8
PW = 32
W = H * PW
S = 128

NN = (((1,), (0,)), ((), ()))
NT = (((1,), (1,)), ((), ()))
TN = (((0,), (0,)), ((), ()))


def split(a):
    high = a.astype(BF16)
    low = (a - high.astype(F32)).astype(BF16)
    return high, low


def dot(a, b, dims=NN):
    return lax.dot_general(a, b, dims, preferred_element_type=F32)


def mm(a, b, dims=NN):
    return dot(a[0], b[0], dims) + (dot(a[0], b[1], dims) + dot(a[1], b[0], dims))


def exact(a, b, dims=NN):
    return lax.dot_general(a, b, dims, precision=HIGHEST, preferred_element_type=F32)


def iota(shape, dim):
    return lax.broadcasted_iota(jnp.int32, shape, dim)


def kernel(
    x_any, b_any, c_any, st_any, rate_any, g_any,
    gx_ref, gb_ref, gc_ref, gs_ref,
    x_ref, b_ref, c_ref, st_ref, rate_ref, g_ref,
    dec, decs, before_z, after_z, across, across_y,
    send_s, send_a, recv_s, recv_a, sum_s, sum_a, sum_sy, sum_ay, out_s, out_a, in_s, in_a,
    sems, rems, loads,
):
    me = lax.axis_index("ctx")
    px, py, pz = me // 16, (me // 8) % 2, me % 8
    mine = px * Z + pz
    x_at = [lax.rem(px + k, X) for k in range(X)]
    z_at = [lax.rem(pz + k, Z) for k in range(Z)]
    partner = px * 16 + (1 - py) * 8 + pz
    far_x, far_z = (2, 1, 3, 0), (4, 3, 5, 2, 6, 1, 7, 0)
    by_x = [(x_at[x] * 16 + py * 8 + z_at[z], x_at[x] * Z + z_at[z]) for x in far_x for z in far_z]
    by_z = [(x_at[x] * 16 + py * 8 + z_at[z], x_at[x] * Z + z_at[z]) for z in far_z for x in far_x]
    by_x, by_z = by_x[:-1], by_z[:-1]

    barrier = pltpu.get_barrier_semaphore()
    for to in [partner] + [to for to, _ in by_x]:
        pl.semaphore_signal(barrier, inc=1, device_id={"ctx": to}, device_id_type=MESH)

    operands = (
        (st_any, st_ref), (rate_any, rate_ref), (x_any, x_ref), (b_any, b_ref),
        (g_any, g_ref), (c_any, c_ref),
    )
    copies = [
        pltpu.make_async_copy(there, here, loads.at[k]) for k, (there, here) in enumerate(operands)
    ]
    for copy in copies:
        copy.start()

    def send(source, target, which, to):
        pltpu.make_async_remote_copy(
            src_ref=source,
            dst_ref=target,
            send_sem=sems.at[which],
            recv_sem=rems.at[which],
            device_id={"ctx": to},
            device_id_type=MESH,
        ).start()

    def send_all(source, target, which, peers):
        for to, place in peers:
            send(source.at[place], target.at[mine], which, to)

    def wait(sem, which, some):
        pltpu.make_async_copy(some, some, sem.at[which]).wait()

    def wait_all(sem, which, like):
        wait(sem, which, like.at[pl.ds(0, N - 1)])

    copies[0].wait()
    copies[1].wait()
    head = iota((H, T), 0)
    rate = jnp.zeros((H, T), F32)
    for h in range(H):
        rate = jnp.where(head == h, rate_ref[h], rate)
    row_t, col_t = iota((T, T), 0), iota((T, T), 1)
    tri = (col_t <= row_t).astype(F32)
    sel32 = (iota((H, W), 1) // PW == iota((H, W), 0)).astype(F32)
    cum, from_start, to_end = [], [], []
    for i in range(2):
        logd = -rate * st_ref[0, i]
        total = jnp.exp(jnp.sum(logd, axis=1, keepdims=True))
        for h in range(H):
            dec[h, pl.ds(i, 1), :] = jnp.broadcast_to(total[h : h + 1], (1, S))
        cum_i = exact(tri, logd, NT)
        wide = exact(cum_i, sel32)
        cum.append(cum_i)
        from_start.append(jnp.exp(wide))
        to_end.append(jnp.exp(wide[T - 1 : T] - wide))
    decs[mine] = dec[mine // 4]

    xw, gw, bs, cs, xs, gs = [], [], [], [], [], []
    copies[2].wait()
    copies[3].wait()
    for i in range(2):
        x, b = x_ref[0, i], b_ref[0, i]
        xs.append(split(x))
        bs.append(split(b))
        xw.append(split(x * to_end[i]))
        send_s[:, 8 * i : 8 * i + 8, :] = mm(xw[i], bs[i], TN).reshape(N, 8, S)
    recv_s[mine] = send_s[mine]

    pl.semaphore_wait(barrier, N)
    for to, place in by_x:
        send(dec.at[place // 4], decs.at[mine], 0, to)
    send_all(send_s, recv_s, 1, by_x)

    copies[4].wait()
    copies[5].wait()
    for i in range(2):
        g, c = g_ref[0, i], c_ref[0, i]
        gs.append(split(g))
        cs.append(split(c))
        gw.append(split(g * from_start[i]))
        send_a[:, 8 * i : 8 * i + 8, :] = mm(gw[i], cs[i], TN).reshape(N, 8, S)
    recv_a[mine] = send_a[mine]
    send_all(send_a, recv_a, 2, by_x)

    lane_head = iota((T, W), 1) // PW
    t_wide, s_wide = iota((T, H * T), 0), iota((T, H * T), 1) % T
    sel64 = (iota((H, H * T), 1) // T == iota((H, H * T), 0)).astype(F32)
    pick = (iota((H * T, H), 0) // T == iota((H * T, H), 1)).astype(BF16)
    pick32 = (iota((W, H), 0) // PW == iota((W, H), 1)).astype(BF16)
    zero = jnp.zeros((), BF16)

    def stacked(parts):
        return [
            jnp.concatenate([jnp.where(lane_head == h, part, zero) for h in range(H)], axis=0)
            for part in parts
        ]

    def twice(parts):
        return [jnp.concatenate([part, part], axis=0) for part in parts]

    def folded(a):
        return a[:, :128] + a[:, 128:256] + (a[:, 256:384] + a[:, 384:])

    def by_head(a, selection):
        high, low = split(a)
        return dot(high, selection) + dot(low, selection)

    def within(i):
        columns = exact(cum[i], sel64)
        row = jnp.sum(jnp.where(t_wide == s_wide, columns, 0.0), axis=0, keepdims=True)
        gap = columns - row
        forward = jnp.exp(jnp.where(s_wide <= t_wide, gap, -1e30))
        backward = jnp.exp(jnp.where(s_wide >= t_wide, -gap, -1e30))
        b_twice, c_twice = twice(bs[i]), twice(cs[i])
        x_stack, g_stack = stacked(xs[i]), stacked(gs[i])
        scores = jnp.concatenate([mm(cs[i], b_twice, NT)] * 4, axis=1)
        scores_back = jnp.concatenate([mm(bs[i], c_twice, NT)] * 4, axis=1)
        inner = forward * mm(gs[i], x_stack, NT)
        inner_back = backward * mm(xs[i], g_stack, NT)
        gc_ref[0, i] = mm(split(folded(inner)), b_twice)
        gb_ref[0, i] = mm(split(folded(inner_back)), c_twice)
        gx_ref[0, i] = mm(split(scores_back * backward), g_stack)
        off = s_wide != t_wide
        return by_head(jnp.where(off, scores * inner, 0.0), pick) - by_head(
            jnp.where(off, scores_back * inner_back, 0.0), pick
        )

    d_cum = [within(0), None]

    wait_all(rems, 0, decs)
    for x in range(X):
        one = jnp.ones((2, S), F32)
        for z in range(Z):
            before_z[x * Z + z] = one
            one *= decs[x * Z + z]
        across[x] = one
        one = jnp.ones((2, S), F32)
        for z in reversed(range(Z)):
            after_z[x * Z + z] = one
            one *= decs[x * Z + z]
    send(across, across_y, 3, partner)

    def rows(slot):
        return pl.ds(8 * slot, 8)

    def scan(received, result, sums, first):
        for slot, order in ((first, range(Z)), (1 - first, range(Z - 1, -1, -1))):
            carry = [jnp.zeros((8, S), F32)] * X
            for z in order:
                for x in range(X):
                    at = x * Z + z
                    result[at, rows(slot), :] = carry[x]
                    carry[x] = (
                        decs[at, slot : slot + 1, :] * carry[x] + received[at, rows(slot), :]
                    )
            for x in range(X):
                sums[x, rows(slot), :] = carry[x]

    def compose(result, sums, sums_y, first):
        is_low = py == 0

        def planes(ours, theirs, slot):
            pairs = [(ours(x, slot), theirs(x, slot)) for x in range(X)]
            return [
                jnp.where(is_low == (y == 0), a, b) for a, b in pairs for y in range(2)
            ]

        def decay(ref):
            return lambda x, slot: ref[x, slot : slot + 1, :]

        def total(ref):
            return lambda x, slot: ref[x, rows(slot), :]

        carry = jnp.zeros((8, S), F32)
        for slot, order, along in (
            (first, range(2 * X), before_z),
            (1 - first, range(2 * X - 1, -1, -1), after_z),
        ):
            decays = planes(decay(across), decay(across_y), slot)
            totals = planes(total(sums), total(sums_y), slot)
            entering = [None] * (2 * X)
            for p in order:
                entering[p] = carry
                carry = decays[p] * carry + totals[p]
            for x in range(X):
                plane = jnp.where(is_low, entering[2 * x], entering[2 * x + 1])
                for z in range(Z):
                    at = x * Z + z
                    result[at, rows(slot), :] += along[at, slot : slot + 1, :] * plane

    wait_all(rems, 1, recv_s)
    scan(recv_s, out_s, sum_s, 0)
    send(sum_s, sum_sy, 4, partner)
    wait_all(rems, 2, recv_a)
    scan(recv_a, out_a, sum_a, 1)
    send(sum_a, sum_ay, 5, partner)
    wait(rems, 3, across_y)
    wait(rems, 4, sum_sy)
    compose(out_s, sum_s, sum_sy, 0)
    in_s[mine] = out_s[mine]
    send_all(out_s, in_s, 6, by_z)
    wait(rems, 5, sum_ay)
    compose(out_a, sum_a, sum_ay, 1)
    in_a[mine] = out_a[mine]
    send_all(out_a, in_a, 7, by_z)

    d_cum[1] = within(1)

    def unpack(buffer):
        return [buffer[:, 8 * i : 8 * i + 8, :].reshape(W, S) for i in range(2)]

    wait_all(rems, 6, in_s)
    entering = unpack(in_s)
    for i in range(2):
        parts = split(entering[i])
        carried = mm(cs[i], parts, NT)
        gc_ref[0, i] += mm(gw[i], parts)
        d_cum[i] += by_head(g_ref[0, i] * from_start[i] * carried, pick32)
    wait_all(rems, 7, in_a)
    leaving = unpack(in_a)
    after = (row_t >= col_t).astype(F32)
    before = (row_t < col_t).astype(F32)
    for i in range(2):
        parts = split(leaving[i])
        weighted = to_end[i] * mm(bs[i], parts, NT)
        gx_ref[0, i] += weighted
        gb_ref[0, i] += mm(xw[i], parts)
        fresh = by_head(x_ref[0, i] * weighted, pick32)
        ends = exact(sel32, leaving[i] * entering[i])
        through = jnp.sum(ends, axis=1, keepdims=True) * jnp.concatenate(
            [dec[h, pl.ds(i, 1), 0:1] for h in range(H)], axis=0
        )
        d_log = exact(d_cum[i], after, TN) + exact(fresh, before, TN) + through
        gs_ref[0, i] = -rate * d_log

    wait_all(sems, 0, decs)
    wait_all(sems, 1, send_s)
    wait_all(sems, 2, send_a)
    wait(sems, 3, across)
    wait(sems, 4, sum_s)
    wait(sems, 5, sum_a)
    wait_all(sems, 6, out_s)
    wait_all(sems, 7, out_a)


def leave(*refs):
    n = len(refs) // 2
    copies = [
        pltpu.make_async_copy(here, there, refs[-1].at[k])
        for k, (here, there) in enumerate(zip(refs[:n], refs[n : 2 * n]))
    ]
    for copy in copies:
        copy.start()
    for copy in copies:
        copy.wait()


def per_device(inputs, b_matrix, c_matrix, step_sizes, decay_rate, cotangent):
    vmem = pl.BlockSpec(memory_space=pltpu.VMEM)
    hbm = pl.BlockSpec(memory_space=pltpu.HBM)
    chunks = pltpu.VMEM((N, 16, S), F32)
    sums = pltpu.VMEM((X, 16, S), F32)
    outs = [jax.ShapeDtypeStruct(a.shape, F32) for a in (inputs, b_matrix, c_matrix, step_sizes)]
    results = pl.pallas_call(
        kernel,
        name="mirrored_scan",
        out_shape=outs,
        in_specs=[hbm] * 6,
        out_specs=[vmem] * 4,
        scratch_shapes=[
            *[pltpu.VMEM(a.shape, F32) for a in (inputs, b_matrix, c_matrix, step_sizes)],
            pltpu.SMEM(decay_rate.shape, F32),
            pltpu.VMEM(cotangent.shape, F32),
            pltpu.VMEM((H, 2, S), F32),
            *[pltpu.VMEM((N, 2, S), F32)] * 3,
            *[pltpu.VMEM((X, 2, S), F32)] * 2,
            *[chunks] * 4,
            *[sums] * 4,
            *[chunks] * 4,
            pltpu.SemaphoreType.DMA((8,)),
            pltpu.SemaphoreType.DMA((8,)),
            pltpu.SemaphoreType.DMA((6,)),
        ],
        compiler_params=pltpu.CompilerParams(
            collective_id=0, has_side_effects=True, vmem_limit_bytes=60 << 20
        ),
    )(inputs, b_matrix, c_matrix, step_sizes, decay_rate, cotangent)
    return pl.pallas_call(
        leave,
        name="leave",
        out_shape=outs,
        in_specs=[vmem] * 4,
        out_specs=[hbm] * 4,
        scratch_shapes=[pltpu.SemaphoreType.DMA((4,))],
    )(*results)


def solution(mesh):
    blocks = P("ctx", None, None, "tp")
    steps = P("ctx", None, "tp", None)
    return jax.shard_map(
        per_device,
        mesh=mesh,
        in_specs=(blocks, blocks, blocks, steps, P("tp"), blocks),
        out_specs=(blocks, blocks, blocks, steps),
        check_vma=False,
    )
```

```python
import functools

import jax
import jax.numpy as jnp
from jax import lax
from jax.experimental import pallas as pl
from jax.experimental.pallas import tpu as pltpu
from jax.sharding import PartitionSpec as P

F32 = jnp.float32
BF16 = jnp.bfloat16
HIGHEST = lax.Precision.HIGHEST
MESH = pl.DeviceIdType.MESH

Z = 8
X, Y = 4, 2
PIECES = 4
PART = 16
T = 64
H = 8
PW = 32
W = H * PW
S = 128

NN = (((1,), (0,)), ((), ()))
NT = (((1,), (1,)), ((), ()))
TN = (((0,), (0,)), ((), ()))


def split(a):
    high = a.astype(BF16)
    low = (a - high.astype(F32)).astype(BF16)
    return high, low


def dot(a, b, dims=NN):
    return lax.dot_general(a, b, dims, preferred_element_type=F32)


def mm(a, b, dims=NN):
    return dot(a[0], b[0], dims) + (dot(a[0], b[1], dims) + dot(a[1], b[0], dims))


def rows_mm(a, b, dims=NN):
    n = a[0].shape[0]
    both = dot(jnp.concatenate(a, axis=0), b[0], dims)
    return both[:n] + (both[n:] + dot(a[0], b[1], dims))


def exact(a, b, dims=NN):
    return lax.dot_general(a, b, dims, precision=HIGHEST, preferred_element_type=F32)


def iota(shape, dim):
    return lax.broadcasted_iota(jnp.int32, shape, dim)


def kernel(
    x_any, b_any, c_any, st_any, rate_any, g_any,
    gx_ref, gb_ref, gc_ref, gs_ref,
    x_ref, b_ref, c_ref, st_ref, rate_ref, g_ref,
    dec, decs, before_z, after_z, line_decs, outgoing, arrived, line_sums, result, returned,
    sems, rems, loads,
):
    me = lax.axis_index("ctx")
    line, pz = me // Z, me % Z
    px, py = line // Y, line % Y
    z_at = [lax.rem(pz + k, Z) for k in (4, 3, 5, 2, 6, 1, 7)]
    lines = [
        lax.rem(px + x, X) * Y + lax.rem(py + y, Y) for y in (1, 0) for x in (2, 1, 3, 0)
    ][:-1]

    barrier = pltpu.get_barrier_semaphore()
    for to in [other * Z + pz for other in lines] + [line * Z + z for z in z_at]:
        pl.semaphore_signal(barrier, inc=1, device_id={"ctx": to}, device_id_type=MESH)

    operands = (
        (st_any, st_ref), (rate_any, rate_ref), (x_any, x_ref), (b_any, b_ref),
        (g_any, g_ref), (c_any, c_ref),
    )
    copies = [
        pltpu.make_async_copy(there, here, loads.at[k]) for k, (there, here) in enumerate(operands)
    ]
    for copy in copies:
        copy.start()

    def send(source, target, which, to):
        pltpu.make_async_remote_copy(
            src_ref=source,
            dst_ref=target,
            send_sem=sems.at[which],
            recv_sem=rems.at[which],
            device_id={"ctx": to},
            device_id_type=MESH,
        ).start()

    def wait(sem, which, like):
        some = like.at[pl.ds(0, 7)]
        pltpu.make_async_copy(some, some, sem.at[which]).wait()

    TO_OWNER, TO_LINES, BACK = 2, 2 + PIECES, 2 + 2 * PIECES

    copies[0].wait()
    copies[1].wait()
    head = iota((H, T), 0)
    rate = jnp.zeros((H, T), F32)
    for h in range(H):
        rate = jnp.where(head == h, rate_ref[h], rate)
    row_t, col_t = iota((T, T), 0), iota((T, T), 1)
    tri = (col_t <= row_t).astype(F32)
    sel32 = (iota((H, W), 1) // PW == iota((H, W), 0)).astype(F32)
    cum, from_start, to_end = [], [], []
    for i in range(2):
        logd = -rate * st_ref[0, i]
        total = jnp.exp(jnp.sum(logd, axis=1, keepdims=True))
        for h in range(H):
            dec[h, pl.ds(i, 1), :] = jnp.broadcast_to(total[h : h + 1], (1, S))
        cum_i = exact(tri, logd, NT)
        wide = exact(cum_i, sel32)
        cum.append(cum_i)
        from_start.append(jnp.exp(wide))
        to_end.append(jnp.exp(wide[T - 1 : T] - wide))
    decs[pz] = dec[pz]

    xw, gw, bs, cs, xs, gs = [], [], [], [], [], []

    def slot_rows(i):
        return slice(PART * i, PART * i + PART)

    def pack(state, i, first_piece):
        heads = state.reshape(H, PW, S)
        for part in range(2):
            outgoing[first_piece + part, :, slot_rows(i), :] = heads[:, slot_rows(part)]

    def to_owners(k):
        arrived[k, pz] = outgoing[k, pz]
        for z in z_at:
            send(outgoing.at[k, z], arrived.at[k, pz], TO_OWNER + k, line * Z + z)

    copies[2].wait()
    copies[3].wait()
    for i in range(2):
        x, b = x_ref[0, i], b_ref[0, i]
        xs.append(split(x))
        bs.append(split(b))
        xw.append(split(x * to_end[i]))
        pack(mm(xw[i], bs[i], TN), i, 0)

    pl.semaphore_wait(barrier, 14)
    for z in z_at:
        send(dec.at[z], decs.at[pz], 0, line * Z + z)
    to_owners(0)
    to_owners(1)

    copies[4].wait()
    copies[5].wait()
    for i in range(2):
        g, c = g_ref[0, i], c_ref[0, i]
        gs.append(split(g))
        cs.append(split(c))
        gw.append(split(g * from_start[i]))
        pack(mm(gw[i], cs[i], TN), i, 2)
    to_owners(2)

    lane_head = iota((T, W), 1) // PW
    t_wide, s_wide = iota((T, H * T), 0), iota((T, H * T), 1) % T
    sel64 = (iota((H, H * T), 1) // T == iota((H, H * T), 0)).astype(F32)
    pick = (iota((H * T, H), 0) // T == iota((H * T, H), 1)).astype(BF16)
    pick32 = (iota((W, H), 0) // PW == iota((W, H), 1)).astype(BF16)
    zero = jnp.zeros((), BF16)

    def stacked(parts):
        return [
            jnp.concatenate([jnp.where(lane_head == h, part, zero) for h in range(H)], axis=0)
            for part in parts
        ]

    def twice(parts):
        return [jnp.concatenate([part, part], axis=0) for part in parts]

    def folded(a):
        return a[:, :128] + a[:, 128:256] + (a[:, 256:384] + a[:, 384:])

    def by_head(a, selection):
        high, low = split(a)
        return dot(high, selection) + dot(low, selection)

    def within(i):
        columns = exact(cum[i], sel64)
        row = jnp.sum(jnp.where(t_wide == s_wide, columns, 0.0), axis=0, keepdims=True)
        gap = columns - row
        forward = jnp.exp(jnp.where(s_wide <= t_wide, gap, -1e30))
        backward = jnp.exp(jnp.where(s_wide >= t_wide, -gap, -1e30))
        b_twice, c_twice = twice(bs[i]), twice(cs[i])
        x_stack, g_stack = stacked(xs[i]), stacked(gs[i])
        scores = jnp.concatenate([mm(cs[i], b_twice, NT)] * 4, axis=1)
        scores_back = jnp.concatenate([mm(bs[i], c_twice, NT)] * 4, axis=1)
        inner = forward * mm(gs[i], x_stack, NT)
        inner_back = backward * mm(xs[i], g_stack, NT)
        gc_ref[0, i] = mm(split(folded(inner)), b_twice)
        gb_ref[0, i] = mm(split(folded(inner_back)), c_twice)
        gx_ref[0, i] = mm(split(scores_back * backward), g_stack)
        off = s_wide != t_wide
        return by_head(jnp.where(off, scores * inner, 0.0), pick) - by_head(
            jnp.where(off, scores_back * inner_back, 0.0), pick
        )

    def scan(k):
        first = k // 2
        for slot, order in ((first, range(Z)), (1 - first, range(Z - 1, -1, -1))):
            carry = jnp.zeros((PART, S), F32)
            for z in order:
                result[k, z, slot_rows(slot), :] = carry
                carry = decs[z, slot : slot + 1, :] * carry + arrived[k, z, slot_rows(slot), :]
            line_sums[k, line, slot_rows(slot), :] = carry

    def compose(k):
        first = k // 2
        carry = jnp.zeros((PART, S), F32)
        for slot, order, along_z in (
            (first, range(Z), before_z),
            (1 - first, range(Z - 1, -1, -1), after_z),
        ):
            enters = jnp.zeros((PART, S), F32)
            for p in order:
                enters = jnp.where(line == p, carry, enters)
                carry = (
                    line_decs[p, slot : slot + 1, :] * carry + line_sums[k, p, slot_rows(slot), :]
                )
            for z in range(Z):
                result[k, z, slot_rows(slot), :] += along_z[z, slot : slot + 1, :] * enters

    def to_lines(k):
        wait(rems, TO_OWNER + k, arrived.at[k])
        scan(k)
        for other in lines:
            send(
                line_sums.at[k, line], line_sums.at[k, line], TO_LINES + k, other * Z + pz
            )

    def back(k):
        wait(rems, TO_LINES + k, line_sums.at[k])
        compose(k)
        returned[k, pz] = result[k, pz]

        def to(z):
            send(result.at[k, z], returned.at[k, pz], BACK + k, line * Z + z)

        pl.when(pz != 0)(lambda: to(0))
        for z in z_at:
            pl.when(z != 0)(functools.partial(to, z))

    d_cum = [within(0), None]

    wait(rems, 0, decs)
    one = jnp.ones((2, S), F32)
    for z in range(Z):
        before_z[z] = one
        one *= decs[z]
    line_decs[line] = one
    one = jnp.ones((2, S), F32)
    for z in reversed(range(Z)):
        after_z[z] = one
        one *= decs[z]
    for other in lines:
        send(line_decs.at[line], line_decs.at[line], 1, other * Z + pz)

    to_lines(0)
    to_owners(3)
    to_lines(1)
    to_lines(2)
    wait(rems, 1, line_decs)
    back(0)
    to_lines(3)
    back(1)
    back(2)
    back(3)

    d_cum[1] = within(1)

    def unpack(first_piece):
        for part in range(2):
            wait(rems, BACK + first_piece + part, returned.at[first_piece + part])
        return [
            jnp.concatenate(
                [returned[first_piece + part, :, slot_rows(i), :] for part in range(2)], axis=1
            ).reshape(W, S)
            for i in range(2)
        ]

    after = (row_t >= col_t).astype(F32)
    before = (row_t < col_t).astype(BF16)

    def along(a, triangle):
        return sum(dot(part, triangle, TN) for part in split(a))

    entering = unpack(0)
    d_log = []
    for i in range(2):
        parts = split(entering[i])
        carried = rows_mm(cs[i], parts, NT)
        gc_ref[0, i] += rows_mm(gw[i], parts)
        d_cum[i] += by_head(g_ref[0, i] * from_start[i] * carried, pick32)
        d_log.append(exact(d_cum[i], after, TN))
    ends = [
        jnp.concatenate([dec[h, pl.ds(i, 1), 0:1] for h in range(H)], axis=0) for i in range(2)
    ]
    leaving = unpack(2)
    for i in range(2):
        parts = split(leaving[i])
        weighted = to_end[i] * rows_mm(bs[i], parts, NT)
        gx_ref[0, i] += weighted
        gb_ref[0, i] += rows_mm(xw[i], parts)
        fresh = by_head(x_ref[0, i] * weighted, pick32)
        product = jnp.sum((leaving[i] * entering[i]).reshape(H, PW, S), axis=1)
        through = jnp.sum(product, axis=1, keepdims=True) * ends[i]
        gs_ref[0, i] = -rate * (d_log[i] + along(fresh, before) + through)

    wait(sems, 0, decs)
    wait(sems, 1, line_decs)
    for k in range(PIECES):
        wait(sems, TO_OWNER + k, outgoing.at[k])
        wait(sems, TO_LINES + k, line_sums.at[k])
        wait(sems, BACK + k, result.at[k])


def leave(*refs):
    n = len(refs) // 2
    copies = [
        pltpu.make_async_copy(here, there, refs[-1].at[k])
        for k, (here, there) in enumerate(zip(refs[:n], refs[n : 2 * n]))
    ]
    for copy in copies:
        copy.start()
    for copy in copies:
        copy.wait()


def per_device(inputs, b_matrix, c_matrix, step_sizes, decay_rate, cotangent):
    vmem = pl.BlockSpec(memory_space=pltpu.VMEM)
    hbm = pl.BlockSpec(memory_space=pltpu.HBM)
    decays = pltpu.VMEM((8, 2, S), F32)
    chunks = pltpu.VMEM((PIECES, 8, 2 * PART, S), F32)
    n_sems = 2 + 3 * PIECES
    outs = [jax.ShapeDtypeStruct(a.shape, F32) for a in (inputs, b_matrix, c_matrix, step_sizes)]
    results = pl.pallas_call(
        kernel,
        name="mirrored_scan",
        out_shape=outs,
        in_specs=[hbm] * 6,
        out_specs=[vmem] * 4,
        scratch_shapes=[
            *[pltpu.VMEM(a.shape, F32) for a in (inputs, b_matrix, c_matrix, step_sizes)],
            pltpu.SMEM(decay_rate.shape, F32),
            pltpu.VMEM(cotangent.shape, F32),
            *[decays] * 5,
            *[chunks] * 5,
            pltpu.SemaphoreType.DMA((n_sems,)),
            pltpu.SemaphoreType.DMA((n_sems,)),
            pltpu.SemaphoreType.DMA((6,)),
        ],
        compiler_params=pltpu.CompilerParams(
            collective_id=0, has_side_effects=True, vmem_limit_bytes=60 << 20
        ),
    )(inputs, b_matrix, c_matrix, step_sizes, decay_rate, cotangent)
    return pl.pallas_call(
        leave,
        name="leave",
        out_shape=outs,
        in_specs=[vmem] * 4,
        out_specs=[hbm] * 4,
        scratch_shapes=[pltpu.SemaphoreType.DMA((4,))],
    )(*results)


def solution(mesh):
    blocks = P("ctx", None, None, "tp")
    steps = P("ctx", None, "tp", None)
    return jax.shard_map(
        per_device,
        mesh=mesh,
        in_specs=(blocks, blocks, blocks, steps, P("tp"), blocks),
        out_specs=(blocks, blocks, blocks, steps),
        check_vma=False,
    )
```

```python
import functools

import jax
import jax.numpy as jnp
from jax import lax
from jax.experimental import pallas as pl
from jax.experimental.pallas import tpu as pltpu
from jax.sharding import PartitionSpec as P

F32 = jnp.float32
BF16 = jnp.bfloat16
HIGHEST = lax.Precision.HIGHEST
MESH = pl.DeviceIdType.MESH

Z = 8
X, Y = 4, 2
PIECES = 4
SLOTS = (0, 1, 1, 0)
T = 64
H = 8
PW = 32
W = H * PW
S = 128

NN = (((1,), (0,)), ((), ()))
NT = (((1,), (1,)), ((), ()))
TN = (((0,), (0,)), ((), ()))


def split(a):
    high = a.astype(BF16)
    low = (a - high.astype(F32)).astype(BF16)
    return high, low


def dot(a, b, dims=NN):
    return lax.dot_general(a, b, dims, preferred_element_type=F32)


def mm(a, b, dims=NN):
    return dot(a[0], b[0], dims) + (dot(a[0], b[1], dims) + dot(a[1], b[0], dims))


def rows_mm(a, b, dims=NN):
    n = a[0].shape[0]
    both = dot(jnp.concatenate(a, axis=0), b[0], dims)
    return both[:n] + (both[n:] + dot(a[0], b[1], dims))


def exact(a, b, dims=NN):
    return lax.dot_general(a, b, dims, precision=HIGHEST, preferred_element_type=F32)


def iota(shape, dim):
    return lax.broadcasted_iota(jnp.int32, shape, dim)


def kernel(
    x_any, b_any, c_any, st_any, rate_any, g_any,
    gx_ref, gb_ref, gc_ref, gs_ref,
    x_ref, b_ref, c_ref, st_ref, rate_ref, g_ref,
    dec, decs, before_z, after_z, line_decs, outgoing, arrived, line_sums, result, returned,
    sems, rems, loads,
):
    me = lax.axis_index("ctx")
    line, pz = me // Z, me % Z
    px, py = line // Y, line % Y
    z_at = [lax.rem(pz + k, Z) for k in (4, 3, 5, 2, 6, 1, 7)]
    lines = [
        lax.rem(px + x, X) * Y + lax.rem(py + y, Y) for y in (1, 0) for x in (2, 1, 3, 0)
    ][:-1]

    barrier = pltpu.get_barrier_semaphore()
    for to in [other * Z + pz for other in lines] + [line * Z + z for z in z_at]:
        pl.semaphore_signal(barrier, inc=1, device_id={"ctx": to}, device_id_type=MESH)

    operands = (
        (st_any, st_ref), (rate_any, rate_ref), (x_any, x_ref), (b_any, b_ref),
        (g_any, g_ref), (c_any, c_ref),
    )
    copies = [
        pltpu.make_async_copy(there, here, loads.at[k]) for k, (there, here) in enumerate(operands)
    ]
    for copy in copies:
        copy.start()

    def send(source, target, which, to):
        pltpu.make_async_remote_copy(
            src_ref=source,
            dst_ref=target,
            send_sem=sems.at[which],
            recv_sem=rems.at[which],
            device_id={"ctx": to},
            device_id_type=MESH,
        ).start()

    def wait(sem, which, like):
        some = like.at[pl.ds(0, 7)]
        pltpu.make_async_copy(some, some, sem.at[which]).wait()

    TO_OWNER, TO_LINES, BACK = 2, 2 + PIECES, 2 + 2 * PIECES

    copies[0].wait()
    copies[1].wait()
    head = iota((H, T), 0)
    rate = jnp.zeros((H, T), F32)
    for h in range(H):
        rate = jnp.where(head == h, rate_ref[h], rate)
    row_t, col_t = iota((T, T), 0), iota((T, T), 1)
    tri = (col_t <= row_t).astype(F32)
    sel32 = (iota((H, W), 1) // PW == iota((H, W), 0)).astype(F32)
    cum, from_start, to_end = [], [], []
    for i in range(2):
        logd = -rate * st_ref[0, i]
        total = jnp.exp(jnp.sum(logd, axis=1, keepdims=True))
        for h in range(H):
            dec[h, pl.ds(i, 1), :] = jnp.broadcast_to(total[h : h + 1], (1, S))
        cum_i = exact(tri, logd, NT)
        wide = exact(cum_i, sel32)
        cum.append(cum_i)
        from_start.append(jnp.exp(wide))
        to_end.append(jnp.exp(wide[T - 1 : T] - wide))
    decs[pz] = dec[pz]

    xw, gw, bs, cs, xs, gs = [], [], [], [], [], []

    def to_owners(k):
        arrived[k, pz] = outgoing[k, pz]
        for z in z_at:
            send(outgoing.at[k, z], arrived.at[k, pz], TO_OWNER + k, line * Z + z)

    copies[2].wait()
    copies[3].wait()
    for i in range(2):
        x, b = x_ref[0, i], b_ref[0, i]
        xs.append(split(x))
        bs.append(split(b))
        xw.append(split(x * to_end[i]))
        outgoing[i] = mm(xw[i], bs[i], TN).reshape(H, PW, S)

    pl.semaphore_wait(barrier, 14)
    for z in z_at:
        send(dec.at[z], decs.at[pz], 0, line * Z + z)
    to_owners(0)
    to_owners(1)

    copies[4].wait()
    copies[5].wait()
    for i in range(2):
        g, c = g_ref[0, i], c_ref[0, i]
        gs.append(split(g))
        cs.append(split(c))
        gw.append(split(g * from_start[i]))
        outgoing[3 - i] = mm(gw[i], cs[i], TN).reshape(H, PW, S)
    to_owners(2)

    lane_head = iota((T, W), 1) // PW
    t_wide, s_wide = iota((T, H * T), 0), iota((T, H * T), 1) % T
    sel64 = (iota((H, H * T), 1) // T == iota((H, H * T), 0)).astype(F32)
    pick = (iota((H * T, H), 0) // T == iota((H * T, H), 1)).astype(BF16)
    pick32 = (iota((W, H), 0) // PW == iota((W, H), 1)).astype(BF16)
    zero = jnp.zeros((), BF16)

    def stacked(parts):
        return [
            jnp.concatenate([jnp.where(lane_head == h, part, zero) for h in range(H)], axis=0)
            for part in parts
        ]

    def twice(parts):
        return [jnp.concatenate([part, part], axis=0) for part in parts]

    def folded(a):
        return a[:, :128] + a[:, 128:256] + (a[:, 256:384] + a[:, 384:])

    def by_head(a, selection):
        high, low = split(a)
        return dot(high, selection) + dot(low, selection)

    def within(i):
        columns = exact(cum[i], sel64)
        row = jnp.sum(jnp.where(t_wide == s_wide, columns, 0.0), axis=0, keepdims=True)
        gap = columns - row
        forward = jnp.exp(jnp.where(s_wide <= t_wide, gap, -1e30))
        backward = jnp.exp(jnp.where(s_wide >= t_wide, -gap, -1e30))
        b_twice, c_twice = twice(bs[i]), twice(cs[i])
        x_stack, g_stack = stacked(xs[i]), stacked(gs[i])
        scores = jnp.concatenate([mm(cs[i], b_twice, NT)] * 4, axis=1)
        scores_back = jnp.concatenate([mm(bs[i], c_twice, NT)] * 4, axis=1)
        inner = forward * mm(gs[i], x_stack, NT)
        inner_back = backward * mm(xs[i], g_stack, NT)
        gc_ref[0, i] = mm(split(folded(inner)), b_twice)
        gb_ref[0, i] = mm(split(folded(inner_back)), c_twice)
        gx_ref[0, i] = mm(split(scores_back * backward), g_stack)
        off = s_wide != t_wide
        return by_head(jnp.where(off, scores * inner, 0.0), pick) - by_head(
            jnp.where(off, scores_back * inner_back, 0.0), pick
        )

    def scan(k):
        slot = SLOTS[k]
        carry = jnp.zeros((PW, S), F32)
        for z in range(Z) if k % 2 == 0 else range(Z - 1, -1, -1):
            result[k, z] = carry
            carry = decs[z, slot : slot + 1, :] * carry + arrived[k, z]
        line_sums[k, line] = carry

    def compose(k, carry):
        slot = SLOTS[k]
        along_z = before_z if k % 2 == 0 else after_z
        enters = jnp.zeros((PW, S), F32)
        for p in range(Z) if k % 2 == 0 else range(Z - 1, -1, -1):
            enters = jnp.where(line == p, carry, enters)
            carry = line_decs[p, slot : slot + 1, :] * carry + line_sums[k, p]
        for z in range(Z):
            result[k, z] += along_z[z, slot : slot + 1, :] * enters
        return carry

    def to_lines(k):
        wait(rems, TO_OWNER + k, arrived.at[k])
        scan(k)
        for other in lines:
            send(
                line_sums.at[k, line], line_sums.at[k, line], TO_LINES + k, other * Z + pz
            )

    def back(k, carry):
        wait(rems, TO_LINES + k, line_sums.at[k])
        carry = compose(k, carry)
        returned[k, pz] = result[k, pz]

        def to(z):
            send(result.at[k, z], returned.at[k, pz], BACK + k, line * Z + z)

        pl.when(pz != 0)(lambda: to(0))
        for z in z_at:
            pl.when(z != 0)(functools.partial(to, z))
        return carry

    d_cum = [within(0), None]

    wait(rems, 0, decs)
    one = jnp.ones((2, S), F32)
    for z in range(Z):
        before_z[z] = one
        one *= decs[z]
    line_decs[line] = one
    one = jnp.ones((2, S), F32)
    for z in reversed(range(Z)):
        after_z[z] = one
        one *= decs[z]
    for other in lines:
        send(line_decs.at[line], line_decs.at[line], 1, other * Z + pz)

    to_lines(0)
    to_owners(3)
    to_lines(1)
    to_lines(2)
    to_lines(3)
    wait(rems, 1, line_decs)
    nothing = jnp.zeros((PW, S), F32)
    middle = back(0, nothing)
    back(1, middle)
    middle = back(2, nothing)
    back(3, middle)

    d_cum[1] = within(1)

    def unpack(k):
        wait(rems, BACK + k, returned.at[k])
        return returned[k].reshape(W, S)

    after = (row_t >= col_t).astype(F32)
    before = (row_t < col_t).astype(BF16)

    def along(a, triangle):
        return sum(dot(part, triangle, TN) for part in split(a))

    entering, d_log = [], []
    for i in range(2):
        entering.append(unpack(i))
        parts = split(entering[i])
        carried = rows_mm(cs[i], parts, NT)
        gc_ref[0, i] += rows_mm(gw[i], parts)
        d_cum[i] += by_head(g_ref[0, i] * from_start[i] * carried, pick32)
        d_log.append(exact(d_cum[i], after, TN))
    ends = [
        jnp.concatenate([dec[h, pl.ds(i, 1), 0:1] for h in range(H)], axis=0) for i in range(2)
    ]
    for i in (1, 0):
        leaving = unpack(3 - i)
        parts = split(leaving)
        weighted = to_end[i] * rows_mm(bs[i], parts, NT)
        gx_ref[0, i] += weighted
        gb_ref[0, i] += rows_mm(xw[i], parts)
        fresh = by_head(x_ref[0, i] * weighted, pick32)
        product = jnp.sum((leaving * entering[i]).reshape(H, PW, S), axis=1)
        through = jnp.sum(product, axis=1, keepdims=True) * ends[i]
        gs_ref[0, i] = -rate * (d_log[i] + along(fresh, before) + through)

    wait(sems, 0, decs)
    wait(sems, 1, line_decs)
    for k in range(PIECES):
        wait(sems, TO_OWNER + k, outgoing.at[k])
        wait(sems, TO_LINES + k, line_sums.at[k])
        wait(sems, BACK + k, result.at[k])


def leave(*refs):
    n = len(refs) // 2
    copies = [
        pltpu.make_async_copy(here, there, refs[-1].at[k])
        for k, (here, there) in enumerate(zip(refs[:n], refs[n : 2 * n]))
    ]
    for copy in copies:
        copy.start()
    for copy in copies:
        copy.wait()


def per_device(inputs, b_matrix, c_matrix, step_sizes, decay_rate, cotangent):
    vmem = pl.BlockSpec(memory_space=pltpu.VMEM)
    hbm = pl.BlockSpec(memory_space=pltpu.HBM)
    decays = pltpu.VMEM((8, 2, S), F32)
    chunks = pltpu.VMEM((PIECES, 8, PW, S), F32)
    n_sems = 2 + 3 * PIECES
    outs = [jax.ShapeDtypeStruct(a.shape, F32) for a in (inputs, b_matrix, c_matrix, step_sizes)]
    results = pl.pallas_call(
        kernel,
        name="mirrored_scan",
        out_shape=outs,
        in_specs=[hbm] * 6,
        out_specs=[vmem] * 4,
        scratch_shapes=[
            *[pltpu.VMEM(a.shape, F32) for a in (inputs, b_matrix, c_matrix, step_sizes)],
            pltpu.SMEM(decay_rate.shape, F32),
            pltpu.VMEM(cotangent.shape, F32),
            *[decays] * 5,
            *[chunks] * 5,
            pltpu.SemaphoreType.DMA((n_sems,)),
            pltpu.SemaphoreType.DMA((n_sems,)),
            pltpu.SemaphoreType.DMA((6,)),
        ],
        compiler_params=pltpu.CompilerParams(
            collective_id=0, has_side_effects=True, vmem_limit_bytes=60 << 20
        ),
    )(inputs, b_matrix, c_matrix, step_sizes, decay_rate, cotangent)
    return pl.pallas_call(
        leave,
        name="leave",
        out_shape=outs,
        in_specs=[vmem] * 4,
        out_specs=[hbm] * 4,
        scratch_shapes=[pltpu.SemaphoreType.DMA((4,))],
    )(*results)


def solution(mesh):
    blocks = P("ctx", None, None, "tp")
    steps = P("ctx", None, "tp", None)
    return jax.shard_map(
        per_device,
        mesh=mesh,
        in_specs=(blocks, blocks, blocks, steps, P("tp"), blocks),
        out_specs=(blocks, blocks, blocks, steps),
        check_vma=False,
    )
```

```python
import functools

import jax
import jax.numpy as jnp
from jax import lax
from jax.experimental import pallas as pl
from jax.experimental.pallas import tpu as pltpu
from jax.sharding import PartitionSpec as P

F32 = jnp.float32
BF16 = jnp.bfloat16
HIGHEST = lax.Precision.HIGHEST
MESH = pl.DeviceIdType.MESH

Z = 8
X, Y = 4, 2
PIECES = 4
SLOTS = (0, 1, 1, 0)
T = 64
H = 8
PW = 32
W = H * PW
S = 128

NN = (((1,), (0,)), ((), ()))
NT = (((1,), (1,)), ((), ()))
TN = (((0,), (0,)), ((), ()))


def split(a):
    high = a.astype(BF16)
    low = (a - high.astype(F32)).astype(BF16)
    return high, low


def dot(a, b, dims=NN):
    return lax.dot_general(a, b, dims, preferred_element_type=F32)


def mm(a, b, dims=NN):
    return dot(a[0], b[0], dims) + (dot(a[0], b[1], dims) + dot(a[1], b[0], dims))


def rows_mm(a, b, dims=NN):
    n = a[0].shape[0]
    both = dot(jnp.concatenate(a, axis=0), b[0], dims)
    return both[:n] + (both[n:] + dot(a[0], b[1], dims))


def exact(a, b, dims=NN):
    return lax.dot_general(a, b, dims, precision=HIGHEST, preferred_element_type=F32)


def iota(shape, dim):
    return lax.broadcasted_iota(jnp.int32, shape, dim)


def kernel(
    x_any, b_any, c_any, st_any, rate_any, g_any,
    gx_ref, gb_ref, gc_ref, gs_ref,
    x_ref, b_ref, c_ref, st_ref, rate_ref, g_ref,
    dec, decs, before_z, after_z, line_decs, outgoing, arrived, line_sums, result, returned,
    sems, rems, loads,
):
    me = lax.axis_index("ctx")
    line, pz = me // Z, me % Z
    px, py = line // Y, line % Y
    z_at = [lax.rem(pz + k, Z) for k in (4, 5, 3, 6, 2, 7, 1)]
    lines = [
        lax.rem(px + x, X) * Y + lax.rem(py + y, Y) for y in (1, 0) for x in (2, 1, 3, 0)
    ][:-1]

    barrier = pltpu.get_barrier_semaphore()
    for to in [other * Z + pz for other in lines] + [line * Z + z for z in z_at]:
        pl.semaphore_signal(barrier, inc=1, device_id={"ctx": to}, device_id_type=MESH)

    operands = (
        (st_any, st_ref), (rate_any, rate_ref), (x_any, x_ref), (b_any, b_ref),
        (g_any, g_ref), (c_any, c_ref),
    )
    copies = [
        pltpu.make_async_copy(there, here, loads.at[k]) for k, (there, here) in enumerate(operands)
    ]
    for copy in copies:
        copy.start()

    def send(source, target, which, to):
        pltpu.make_async_remote_copy(
            src_ref=source,
            dst_ref=target,
            send_sem=sems.at[which],
            recv_sem=rems.at[which],
            device_id={"ctx": to},
            device_id_type=MESH,
        ).start()

    def wait(sem, which, like):
        some = like.at[pl.ds(0, 7)]
        pltpu.make_async_copy(some, some, sem.at[which]).wait()

    TO_OWNER, TO_LINES, BACK = 2, 2 + PIECES, 2 + 2 * PIECES

    copies[0].wait()
    copies[1].wait()
    head = iota((H, T), 0)
    rate = jnp.zeros((H, T), F32)
    for h in range(H):
        rate = jnp.where(head == h, rate_ref[h], rate)
    row_t, col_t = iota((T, T), 0), iota((T, T), 1)
    tri = (col_t <= row_t).astype(F32)
    sel32 = (iota((H, W), 1) // PW == iota((H, W), 0)).astype(F32)
    cum, from_start, to_end = [], [], []
    for i in range(2):
        logd = -rate * st_ref[0, i]
        total = jnp.exp(jnp.sum(logd, axis=1, keepdims=True))
        for h in range(H):
            dec[h, pl.ds(i, 1), :] = jnp.broadcast_to(total[h : h + 1], (1, S))
        cum_i = exact(tri, logd, NT)
        wide = exact(cum_i, sel32)
        cum.append(cum_i)
        from_start.append(jnp.exp(wide))
        to_end.append(jnp.exp(wide[T - 1 : T] - wide))
    decs[pz] = dec[pz]

    xw, gw, bs, cs, xs, gs = [], [], [], [], [], []

    def to_owners(k):
        arrived[k, pz] = outgoing[k, pz]
        for z in z_at:
            send(outgoing.at[k, z], arrived.at[k, pz], TO_OWNER + k, line * Z + z)

    copies[2].wait()
    copies[3].wait()
    for i in range(2):
        x, b = x_ref[0, i], b_ref[0, i]
        xs.append(split(x))
        bs.append(split(b))
        xw.append(split(x * to_end[i]))
        outgoing[i] = mm(xw[i], bs[i], TN).reshape(H, PW, S)

    pl.semaphore_wait(barrier, 14)
    for z in z_at:
        send(dec.at[z], decs.at[pz], 0, line * Z + z)
    to_owners(0)
    to_owners(1)

    copies[4].wait()
    copies[5].wait()
    for i in range(2):
        g, c = g_ref[0, i], c_ref[0, i]
        gs.append(split(g))
        cs.append(split(c))
        gw.append(split(g * from_start[i]))
        outgoing[3 - i] = mm(gw[i], cs[i], TN).reshape(H, PW, S)
    to_owners(2)

    lane_head = iota((T, W), 1) // PW
    t_wide, s_wide = iota((T, H * T), 0), iota((T, H * T), 1) % T
    sel64 = (iota((H, H * T), 1) // T == iota((H, H * T), 0)).astype(F32)
    pick = (iota((H * T, H), 0) // T == iota((H * T, H), 1)).astype(BF16)
    pick32 = (iota((W, H), 0) // PW == iota((W, H), 1)).astype(BF16)
    zero = jnp.zeros((), BF16)

    def stacked(parts):
        return [
            jnp.concatenate([jnp.where(lane_head == h, part, zero) for h in range(H)], axis=0)
            for part in parts
        ]

    def twice(parts):
        return [jnp.concatenate([part, part], axis=0) for part in parts]

    def folded(a):
        return a[:, :128] + a[:, 128:256] + (a[:, 256:384] + a[:, 384:])

    def by_head(a, selection):
        high, low = split(a)
        return dot(high, selection) + dot(low, selection)

    def within(i):
        columns = exact(cum[i], sel64)
        row = jnp.sum(jnp.where(t_wide == s_wide, columns, 0.0), axis=0, keepdims=True)
        gap = columns - row
        forward = jnp.exp(jnp.where(s_wide <= t_wide, gap, -1e30))
        backward = jnp.exp(jnp.where(s_wide >= t_wide, -gap, -1e30))
        b_twice, c_twice = twice(bs[i]), twice(cs[i])
        x_stack, g_stack = stacked(xs[i]), stacked(gs[i])
        scores = jnp.concatenate([mm(cs[i], b_twice, NT)] * 4, axis=1)
        scores_back = jnp.concatenate([mm(bs[i], c_twice, NT)] * 4, axis=1)
        inner = forward * mm(gs[i], x_stack, NT)
        inner_back = backward * mm(xs[i], g_stack, NT)
        gc_ref[0, i] = mm(split(folded(inner)), b_twice)
        gb_ref[0, i] = mm(split(folded(inner_back)), c_twice)
        gx_ref[0, i] = mm(split(scores_back * backward), g_stack)
        off = s_wide != t_wide
        return by_head(jnp.where(off, scores * inner, 0.0), pick) - by_head(
            jnp.where(off, scores_back * inner_back, 0.0), pick
        )

    def scan(k):
        slot = SLOTS[k]
        carry = jnp.zeros((PW, S), F32)
        for z in range(Z) if k % 2 == 0 else range(Z - 1, -1, -1):
            result[k, z] = carry
            carry = decs[z, slot : slot + 1, :] * carry + arrived[k, z]
        line_sums[k, line] = carry

    def compose(k, carry):
        slot = SLOTS[k]
        along_z = before_z if k % 2 == 0 else after_z
        enters = jnp.zeros((PW, S), F32)
        for p in range(Z) if k % 2 == 0 else range(Z - 1, -1, -1):
            enters = jnp.where(line == p, carry, enters)
            carry = line_decs[p, slot : slot + 1, :] * carry + line_sums[k, p]
        for z in range(Z):
            result[k, z] += along_z[z, slot : slot + 1, :] * enters
        return carry

    def to_lines(k):
        wait(rems, TO_OWNER + k, arrived.at[k])
        scan(k)
        for other in lines:
            send(
                line_sums.at[k, line], line_sums.at[k, line], TO_LINES + k, other * Z + pz
            )

    def back(k, carry):
        wait(rems, TO_LINES + k, line_sums.at[k])
        carry = compose(k, carry)
        returned[k, pz] = result[k, pz]

        def to(z):
            send(result.at[k, z], returned.at[k, pz], BACK + k, line * Z + z)

        pl.when(pz != 0)(lambda: to(0))
        for z in z_at:
            pl.when(z != 0)(functools.partial(to, z))
        return carry

    d_cum = [within(0), None]

    wait(rems, 0, decs)
    one = jnp.ones((2, S), F32)
    for z in range(Z):
        before_z[z] = one
        one *= decs[z]
    line_decs[line] = one
    one = jnp.ones((2, S), F32)
    for z in reversed(range(Z)):
        after_z[z] = one
        one *= decs[z]
    for other in lines:
        send(line_decs.at[line], line_decs.at[line], 1, other * Z + pz)

    to_lines(0)
    to_owners(3)
    to_lines(1)
    to_lines(2)
    to_lines(3)
    wait(rems, 1, line_decs)
    nothing = jnp.zeros((PW, S), F32)
    middle = back(0, nothing)
    back(1, middle)
    middle = back(2, nothing)
    back(3, middle)

    d_cum[1] = within(1)
    wait(sems, 0, decs)
    wait(sems, 1, line_decs)
    for k in range(PIECES):
        wait(sems, TO_OWNER + k, outgoing.at[k])
        wait(sems, TO_LINES + k, line_sums.at[k])

    def unpack(k):
        wait(rems, BACK + k, returned.at[k])
        return returned[k].reshape(W, S)

    after = (row_t >= col_t).astype(F32)
    before = (row_t < col_t).astype(BF16)

    def along(a, triangle):
        return sum(dot(part, triangle, TN) for part in split(a))

    entering, d_log = [], []
    for i in range(2):
        entering.append(unpack(i))
        parts = split(entering[i])
        carried = rows_mm(cs[i], parts, NT)
        gc_ref[0, i] += rows_mm(gw[i], parts)
        d_cum[i] += by_head(g_ref[0, i] * from_start[i] * carried, pick32)
        d_log.append(exact(d_cum[i], after, TN))
    ends = [
        jnp.concatenate([dec[h, pl.ds(i, 1), 0:1] for h in range(H)], axis=0) for i in range(2)
    ]
    for i in (1, 0):
        leaving = unpack(3 - i)
        parts = split(leaving)
        weighted = to_end[i] * rows_mm(bs[i], parts, NT)
        gx_ref[0, i] += weighted
        gb_ref[0, i] += rows_mm(xw[i], parts)
        fresh = by_head(x_ref[0, i] * weighted, pick32)
        product = jnp.sum((leaving * entering[i]).reshape(H, PW, S), axis=1)
        through = jnp.sum(product, axis=1, keepdims=True) * ends[i]
        gs_ref[0, i] = -rate * (d_log[i] + along(fresh, before) + through)

    for k in range(PIECES):
        wait(sems, BACK + k, result.at[k])


def leave(*refs):
    n = len(refs) // 2
    copies = [
        pltpu.make_async_copy(here, there, refs[-1].at[k])
        for k, (here, there) in enumerate(zip(refs[:n], refs[n : 2 * n]))
    ]
    for copy in copies:
        copy.start()
    for copy in copies:
        copy.wait()


def per_device(inputs, b_matrix, c_matrix, step_sizes, decay_rate, cotangent):
    vmem = pl.BlockSpec(memory_space=pltpu.VMEM)
    hbm = pl.BlockSpec(memory_space=pltpu.HBM)
    decays = pltpu.VMEM((8, 2, S), F32)
    chunks = pltpu.VMEM((PIECES, 8, PW, S), F32)
    n_sems = 2 + 3 * PIECES
    outs = [jax.ShapeDtypeStruct(a.shape, F32) for a in (inputs, b_matrix, c_matrix, step_sizes)]
    results = pl.pallas_call(
        kernel,
        name="mirrored_scan",
        out_shape=outs,
        in_specs=[hbm] * 6,
        out_specs=[vmem] * 4,
        scratch_shapes=[
            *[pltpu.VMEM(a.shape, F32) for a in (inputs, b_matrix, c_matrix, step_sizes)],
            pltpu.SMEM(decay_rate.shape, F32),
            pltpu.VMEM(cotangent.shape, F32),
            *[decays] * 5,
            *[chunks] * 5,
            pltpu.SemaphoreType.DMA((n_sems,)),
            pltpu.SemaphoreType.DMA((n_sems,)),
            pltpu.SemaphoreType.DMA((6,)),
        ],
        compiler_params=pltpu.CompilerParams(
            collective_id=0, has_side_effects=True, vmem_limit_bytes=60 << 20
        ),
    )(inputs, b_matrix, c_matrix, step_sizes, decay_rate, cotangent)
    return pl.pallas_call(
        leave,
        name="leave",
        out_shape=outs,
        in_specs=[vmem] * 4,
        out_specs=[hbm] * 4,
        scratch_shapes=[pltpu.SemaphoreType.DMA((4,))],
    )(*results)


def solution(mesh):
    blocks = P("ctx", None, None, "tp")
    steps = P("ctx", None, "tp", None)
    return jax.shard_map(
        per_device,
        mesh=mesh,
        in_specs=(blocks, blocks, blocks, steps, P("tp"), blocks),
        out_specs=(blocks, blocks, blocks, steps),
        check_vma=False,
    )
```

```python
import functools

import jax
import jax.numpy as jnp
from jax import lax
from jax.experimental import pallas as pl
from jax.experimental.pallas import tpu as pltpu
from jax.sharding import PartitionSpec as P

F32 = jnp.float32
BF16 = jnp.bfloat16
HIGHEST = lax.Precision.HIGHEST
MESH = pl.DeviceIdType.MESH

Z = 8
X, Y = 4, 2
PIECES = 4
SLOTS = (0, 1, 1, 0)
T = 64
H = 8
PW = 32
W = H * PW
S = 128

NN = (((1,), (0,)), ((), ()))
NT = (((1,), (1,)), ((), ()))
TN = (((0,), (0,)), ((), ()))


def split(a):
    high = a.astype(BF16)
    low = (a - high.astype(F32)).astype(BF16)
    return high, low


def dot(a, b, dims=NN):
    return lax.dot_general(a, b, dims, preferred_element_type=F32)


def mm(a, b, dims=NN):
    return dot(a[0], b[0], dims) + (dot(a[0], b[1], dims) + dot(a[1], b[0], dims))


def rows_mm(a, b, dims=NN):
    n = a[0].shape[0]
    both = dot(jnp.concatenate(a, axis=0), b[0], dims)
    return both[:n] + (both[n:] + dot(a[0], b[1], dims))


def exact(a, b, dims=NN):
    return lax.dot_general(a, b, dims, precision=HIGHEST, preferred_element_type=F32)


def iota(shape, dim):
    return lax.broadcasted_iota(jnp.int32, shape, dim)


def kernel(
    x_any, b_any, c_any, st_any, rate_any, g_any,
    gx_ref, gb_ref, gc_ref, gs_ref,
    x_ref, b_ref, c_ref, st_ref, rate_ref, g_ref,
    dec, decs, before_z, after_z, line_decs, outgoing, arrived, line_sums, result, returned,
    sems, rems, loads,
):
    me = lax.axis_index("ctx")
    line, pz = me // Z, me % Z
    px, py = line // Y, line % Y
    z_at = [lax.rem(pz + k, Z) for k in (4, 5, 3, 6, 2, 7, 1)]
    lines = [
        lax.rem(px + x, X) * Y + lax.rem(py + y, Y) for x in (2, 1, 3, 0) for y in (1, 0)
    ][:-1]

    barrier = pltpu.get_barrier_semaphore()
    for to in [other * Z + pz for other in lines] + [line * Z + z for z in z_at]:
        pl.semaphore_signal(barrier, inc=1, device_id={"ctx": to}, device_id_type=MESH)

    operands = (
        (st_any, st_ref), (rate_any, rate_ref), (x_any, x_ref), (b_any, b_ref),
        (g_any, g_ref), (c_any, c_ref),
    )
    copies = [
        pltpu.make_async_copy(there, here, loads.at[k]) for k, (there, here) in enumerate(operands)
    ]
    for copy in copies:
        copy.start()

    def send(source, target, which, to):
        pltpu.make_async_remote_copy(
            src_ref=source,
            dst_ref=target,
            send_sem=sems.at[which],
            recv_sem=rems.at[which],
            device_id={"ctx": to},
            device_id_type=MESH,
        ).start()

    def wait(sem, which, like):
        some = like.at[pl.ds(0, 7)]
        pltpu.make_async_copy(some, some, sem.at[which]).wait()

    TO_OWNER, TO_LINES, BACK = 2, 2 + PIECES, 2 + 2 * PIECES

    copies[0].wait()
    copies[1].wait()
    head = iota((H, T), 0)
    rate = jnp.zeros((H, T), F32)
    for h in range(H):
        rate = jnp.where(head == h, rate_ref[h], rate)
    row_t, col_t = iota((T, T), 0), iota((T, T), 1)
    tri = (col_t <= row_t).astype(F32)
    sel32 = (iota((H, W), 1) // PW == iota((H, W), 0)).astype(F32)
    cum, from_start, to_end = [], [], []
    for i in range(2):
        logd = -rate * st_ref[0, i]
        total = jnp.exp(jnp.sum(logd, axis=1, keepdims=True))
        for h in range(H):
            dec[h, pl.ds(i, 1), :] = jnp.broadcast_to(total[h : h + 1], (1, S))
        cum_i = exact(tri, logd, NT)
        wide = exact(cum_i, sel32)
        cum.append(cum_i)
        from_start.append(jnp.exp(wide))
        to_end.append(jnp.exp(wide[T - 1 : T] - wide))
    decs[pz] = dec[pz]

    xw, gw, bs, cs, xs, gs = [], [], [], [], [], []

    def to_owners(k):
        arrived[k, pz] = outgoing[k, pz]
        for z in z_at:
            send(outgoing.at[k, z], arrived.at[k, pz], TO_OWNER + k, line * Z + z)

    copies[2].wait()
    copies[3].wait()
    for i in range(2):
        x, b = x_ref[0, i], b_ref[0, i]
        xs.append(split(x))
        bs.append(split(b))
        xw.append(split(x * to_end[i]))
        outgoing[i] = mm(xw[i], bs[i], TN).reshape(H, PW, S)

    pl.semaphore_wait(barrier, 14)
    for z in z_at:
        send(dec.at[z], decs.at[pz], 0, line * Z + z)
    to_owners(0)
    to_owners(1)

    copies[4].wait()
    copies[5].wait()
    for i in range(2):
        g, c = g_ref[0, i], c_ref[0, i]
        gs.append(split(g))
        cs.append(split(c))
        gw.append(split(g * from_start[i]))
        outgoing[3 - i] = mm(gw[i], cs[i], TN).reshape(H, PW, S)
    to_owners(2)

    lane_head = iota((T, W), 1) // PW
    t_wide, s_wide = iota((T, H * T), 0), iota((T, H * T), 1) % T
    sel64 = (iota((H, H * T), 1) // T == iota((H, H * T), 0)).astype(F32)
    pick = (iota((H * T, H), 0) // T == iota((H * T, H), 1)).astype(BF16)
    pick32 = (iota((W, H), 0) // PW == iota((W, H), 1)).astype(BF16)
    zero = jnp.zeros((), BF16)

    def stacked(parts):
        return [
            jnp.concatenate([jnp.where(lane_head == h, part, zero) for h in range(H)], axis=0)
            for part in parts
        ]

    def twice(parts):
        return [jnp.concatenate([part, part], axis=0) for part in parts]

    def folded(a):
        return a[:, :128] + a[:, 128:256] + (a[:, 256:384] + a[:, 384:])

    def by_head(a, selection):
        high, low = split(a)
        return dot(high, selection) + dot(low, selection)

    def within(i):
        columns = exact(cum[i], sel64)
        row = jnp.sum(jnp.where(t_wide == s_wide, columns, 0.0), axis=0, keepdims=True)
        gap = columns - row
        forward = jnp.exp(jnp.where(s_wide <= t_wide, gap, -1e30))
        backward = jnp.exp(jnp.where(s_wide >= t_wide, -gap, -1e30))
        b_twice, c_twice = twice(bs[i]), twice(cs[i])
        x_stack, g_stack = stacked(xs[i]), stacked(gs[i])
        scores = jnp.concatenate([mm(cs[i], b_twice, NT)] * 4, axis=1)
        scores_back = jnp.concatenate([mm(bs[i], c_twice, NT)] * 4, axis=1)
        inner = forward * mm(gs[i], x_stack, NT)
        inner_back = backward * mm(xs[i], g_stack, NT)
        gc_ref[0, i] = mm(split(folded(inner)), b_twice)
        gb_ref[0, i] = mm(split(folded(inner_back)), c_twice)
        gx_ref[0, i] = mm(split(scores_back * backward), g_stack)
        off = s_wide != t_wide
        return by_head(jnp.where(off, scores * inner, 0.0), pick) - by_head(
            jnp.where(off, scores_back * inner_back, 0.0), pick
        )

    def scan(k):
        slot = SLOTS[k]
        carry = jnp.zeros((PW, S), F32)
        for z in range(Z) if k % 2 == 0 else range(Z - 1, -1, -1):
            result[k, z] = carry
            carry = decs[z, slot : slot + 1, :] * carry + arrived[k, z]
        line_sums[k, line] = carry

    def compose(k, carry):
        slot = SLOTS[k]
        along_z = before_z if k % 2 == 0 else after_z
        enters = jnp.zeros((PW, S), F32)
        for p in range(Z) if k % 2 == 0 else range(Z - 1, -1, -1):
            enters = jnp.where(line == p, carry, enters)
            carry = line_decs[p, slot : slot + 1, :] * carry + line_sums[k, p]
        for z in range(Z):
            result[k, z] += along_z[z, slot : slot + 1, :] * enters
        return carry

    def to_lines(k):
        wait(rems, TO_OWNER + k, arrived.at[k])
        scan(k)
        for other in lines:
            send(
                line_sums.at[k, line], line_sums.at[k, line], TO_LINES + k, other * Z + pz
            )

    def back(k, carry):
        wait(rems, TO_LINES + k, line_sums.at[k])
        carry = compose(k, carry)
        returned[k, pz] = result[k, pz]

        def to(z):
            send(result.at[k, z], returned.at[k, pz], BACK + k, line * Z + z)

        pl.when(pz != 0)(lambda: to(0))
        for z in z_at:
            pl.when(z != 0)(functools.partial(to, z))
        return carry

    d_cum = [within(0), None]

    wait(rems, 0, decs)
    one = jnp.ones((2, S), F32)
    for z in range(Z):
        before_z[z] = one
        one *= decs[z]
    line_decs[line] = one
    one = jnp.ones((2, S), F32)
    for z in reversed(range(Z)):
        after_z[z] = one
        one *= decs[z]
    for other in lines:
        send(line_decs.at[line], line_decs.at[line], 1, other * Z + pz)

    to_lines(0)
    to_owners(3)
    to_lines(1)
    to_lines(2)
    to_lines(3)
    wait(rems, 1, line_decs)
    nothing = jnp.zeros((PW, S), F32)
    middle = back(0, nothing)
    back(1, middle)
    middle = back(2, nothing)
    back(3, middle)

    d_cum[1] = within(1)
    wait(sems, 0, decs)
    wait(sems, 1, line_decs)
    for k in range(PIECES):
        wait(sems, TO_OWNER + k, outgoing.at[k])
        wait(sems, TO_LINES + k, line_sums.at[k])

    def unpack(k):
        wait(rems, BACK + k, returned.at[k])
        return returned[k].reshape(W, S)

    after = (row_t >= col_t).astype(F32)
    before = (row_t < col_t).astype(BF16)

    def along(a, triangle):
        return sum(dot(part, triangle, TN) for part in split(a))

    entering, d_log = [], []
    for i in range(2):
        entering.append(unpack(i))
        parts = split(entering[i])
        carried = rows_mm(cs[i], parts, NT)
        gc_ref[0, i] += rows_mm(gw[i], parts)
        d_cum[i] += by_head(g_ref[0, i] * from_start[i] * carried, pick32)
        d_log.append(exact(d_cum[i], after, TN))
    ends = [
        jnp.concatenate([dec[h, pl.ds(i, 1), 0:1] for h in range(H)], axis=0) for i in range(2)
    ]
    for i in (1, 0):
        leaving = unpack(3 - i)
        parts = split(leaving)
        weighted = to_end[i] * rows_mm(bs[i], parts, NT)
        gx_ref[0, i] += weighted
        gb_ref[0, i] += rows_mm(xw[i], parts)
        fresh = by_head(x_ref[0, i] * weighted, pick32)
        product = jnp.sum((leaving * entering[i]).reshape(H, PW, S), axis=1)
        through = jnp.sum(product, axis=1, keepdims=True) * ends[i]
        gs_ref[0, i] = -rate * (d_log[i] + along(fresh, before) + through)

    for k in range(PIECES):
        wait(sems, BACK + k, result.at[k])


def leave(*refs):
    n = len(refs) // 2
    copies = [
        pltpu.make_async_copy(here, there, refs[-1].at[k])
        for k, (here, there) in enumerate(zip(refs[:n], refs[n : 2 * n]))
    ]
    for copy in copies:
        copy.start()
    for copy in copies:
        copy.wait()


def per_device(inputs, b_matrix, c_matrix, step_sizes, decay_rate, cotangent):
    vmem = pl.BlockSpec(memory_space=pltpu.VMEM)
    hbm = pl.BlockSpec(memory_space=pltpu.HBM)
    decays = pltpu.VMEM((8, 2, S), F32)
    chunks = pltpu.VMEM((PIECES, 8, PW, S), F32)
    n_sems = 2 + 3 * PIECES
    outs = [jax.ShapeDtypeStruct(a.shape, F32) for a in (inputs, b_matrix, c_matrix, step_sizes)]
    results = pl.pallas_call(
        kernel,
        name="mirrored_scan",
        out_shape=outs,
        in_specs=[hbm] * 6,
        out_specs=[vmem] * 4,
        scratch_shapes=[
            *[pltpu.VMEM(a.shape, F32) for a in (inputs, b_matrix, c_matrix, step_sizes)],
            pltpu.SMEM(decay_rate.shape, F32),
            pltpu.VMEM(cotangent.shape, F32),
            *[decays] * 5,
            *[chunks] * 5,
            pltpu.SemaphoreType.DMA((n_sems,)),
            pltpu.SemaphoreType.DMA((n_sems,)),
            pltpu.SemaphoreType.DMA((6,)),
        ],
        compiler_params=pltpu.CompilerParams(
            collective_id=0, has_side_effects=True, vmem_limit_bytes=60 << 20
        ),
    )(inputs, b_matrix, c_matrix, step_sizes, decay_rate, cotangent)
    return pl.pallas_call(
        leave,
        name="leave",
        out_shape=outs,
        in_specs=[vmem] * 4,
        out_specs=[hbm] * 4,
        scratch_shapes=[pltpu.SemaphoreType.DMA((4,))],
    )(*results)


def solution(mesh):
    blocks = P("ctx", None, None, "tp")
    steps = P("ctx", None, "tp", None)
    return jax.shard_map(
        per_device,
        mesh=mesh,
        in_specs=(blocks, blocks, blocks, steps, P("tp"), blocks),
        out_specs=(blocks, blocks, blocks, steps),
        check_vma=False,
    )
```
